32 devices in a mesh: dom: 8 (over z, core), rows: 4 (over y, x).
Axes of the slice: x: 2, y: 2, z: 4, core: 2. Of those that a mesh axis runs over, the one named last changes fastest.
Arguments:
- features: bfloat16 [16384, 256], P(('dom', 'rows')), may hold values from -6 to 6
- weight: bfloat16 [256, 256], replicated, may hold values from -0.375 to 0.375
- tile_values: bfloat16 [32, 5, 4, 128, 128], P(('dom', 'rows')), may hold values from -0.1875 to 0.1875
- tile_source: int32 [32, 5, 4], P(('dom', 'rows')), may hold values from 0 to 3
- tile_slot: int32 [32, 5, 4], P(('dom', 'rows')), may hold values from 0 to 7
- slot_block: int32 [32, 8], P(('dom', 'rows')), may hold values from 0 to 3
- tile_count: int32 [32, 5], P(('dom', 'rows')), may hold values from 1 to 4
- cotangent: bfloat16 [16384, 256], P(('dom', 'rows')), may hold values from -6 to 6
Outputs:
- activations: bfloat16 [16384, 256], P(('dom', 'rows'))
- feature_grad: bfloat16 [16384, 256], P(('dom', 'rows'))
- weight_grad: float32 [256, 256], replicated
The draws below stay inside these ranges and needn't reach their ends.
Inputs may be any that keep to these rules, and one draw needn't show every extreme that they name: Tiles of index tile_count[g, k] and above at offset index k are padding; their tile_values, tile_source and tile_slot count for nothing.
All inputs are finite; a program needn't handle non-finite values.
Results may differ from the reference program's by a relative error of at most 0.019.
Values may be sent and summed in bfloat16 or wider, within the bound.
A program may use at most 64 MiB of HBM per device.

```python
import jax
import jax.numpy as jnp
from jax import lax

F = 256
BLOCK = 128
BLK_DEV = 4
HALF = 2
TPS = 4
CAP = 2
STEPS = 5
NODES = 16384
N_DOM = 8
N_ROWS = 4
DEVICES = 32


def set_ends(drawn, own_key, least, largest):
    spot = [jax.random.randint(jax.random.fold_in(own_key, axis), (), 0, length) for axis, length in enumerate(drawn.shape)]
    main_axis = drawn.shape.index(max(drawn.shape))
    beside = spot[:main_axis] + [(spot[main_axis] + 1) % drawn.shape[main_axis]] + spot[main_axis + 1:]
    return drawn.at[tuple(spot)].set(least).at[tuple(beside)].set(largest)


def levels(rng, dims, split, least, high):
    level, own = 1.0, jax.random.fold_in(rng, 6)
    for dim, shards_of in split:
        draws = jnp.exp(jax.random.uniform(jax.random.fold_in(own, dim), (shards_of,), jnp.float32, least / len(split), high / len(split)))
        level = level * jnp.repeat(draws, dims[dim] // shards_of).reshape([-1 if axis == dim else 1 for axis in range(len(dims))])
    return level


def centred(own_key, shape, spread, most, split=(), kind=jnp.bfloat16):
    array = jax.random.normal(own_key, shape, jnp.float32) * spread
    if len(split) > 0:
        array = levels(own_key, shape, split, -0.22, 0.18) * array
    return jnp.clip(array, min=-most, max=most).astype(kind)


def setup_inputs(seed: int = 0) -> dict:
    key_of = jax.random.split(jax.random.key(seed), 9)
    features = centred(key_of[0], (NODES, F), 1.0, 6.0, ((0, 32),))
    weight = centred(key_of[1], (F, F), F ** -0.5, 0.375)
    tile_values = centred(key_of[2], (DEVICES, STEPS, TPS, BLOCK, BLOCK), (BLOCK * 8) ** -0.5, 0.1875, ((0, 32),))
    tile_source = set_ends(jax.random.randint(key_of[3], (DEVICES, STEPS, TPS), 0, BLK_DEV), jax.random.fold_in(key_of[3], 1), 0, BLK_DEV - 1).astype(jnp.int32)
    tile_slot = set_ends(jax.random.randint(key_of[4], (DEVICES, STEPS, TPS), 0, N_ROWS * CAP), jax.random.fold_in(key_of[4], 1), 0, (N_ROWS * CAP) - 1).astype(jnp.int32)
    slot_block = set_ends(jax.random.randint(key_of[5], (DEVICES, N_ROWS * CAP), 0, BLK_DEV), jax.random.fold_in(key_of[5], 1), 0, BLK_DEV - 1).astype(jnp.int32)
    tile_count = set_ends(jax.random.randint(key_of[6], (DEVICES, STEPS), 1, TPS + 1), jax.random.fold_in(key_of[6], 1), 1, TPS).astype(jnp.int32)
    cotangent = centred(key_of[7], (NODES, F), 1.0, 6.0, ((0, 32),))
    return {"features": features, "weight": weight, "tile_values": tile_values, "tile_source": tile_source, "tile_slot": tile_slot, "slot_block": slot_block, "tile_count": tile_count, "cotangent": cotangent}


def reference(features, weight, tile_values, tile_source, tile_slot, slot_block, tile_count, cotangent):
    channels = features.shape[1]
    slot_total = N_ROWS * CAP
    blocks = features.reshape(-1, BLOCK, channels)
    values = tile_values.reshape(N_DOM, N_ROWS, STEPS, TPS, BLOCK, BLOCK)
    sources = tile_source.reshape(N_DOM, N_ROWS, STEPS, TPS)
    slot_ids = tile_slot.reshape(N_DOM, N_ROWS, STEPS, TPS)
    targets = slot_block.reshape(N_DOM, N_ROWS, slot_total)
    counts = tile_count.reshape(N_DOM, N_ROWS, STEPS)
    offsets = jnp.arange(STEPS, dtype=jnp.int32) - HALF
    row_ids = jnp.arange(N_ROWS, dtype=jnp.int32)
    tile_ids = jnp.arange(TPS, dtype=jnp.int32)
    slot_owner = jnp.arange(slot_total, dtype=jnp.int32) // CAP

    def layout(dom_index):
        src_dev = ((dom_index + offsets)[None, :] % N_DOM) * N_ROWS + row_ids[:, None]
        src_glob = src_dev[:, :, None] * BLK_DEV + sources[dom_index]
        live_mask = (tile_ids[None, None, :] < counts[dom_index][:, :, None]).astype(jnp.float32)
        flat_slots = slot_ids[dom_index].reshape(N_ROWS, STEPS * TPS)
        tile_target = jnp.take_along_axis(targets[dom_index], flat_slots, axis=1).reshape(N_ROWS, STEPS, TPS)
        dest_local = (slot_ids[dom_index] // CAP) * BLK_DEV + tile_target
        return src_glob.astype(jnp.int32), live_mask, dest_local.astype(jnp.int32)

    def forward_dom(dom_index):
        src_glob, live_mask, dest_local = layout(dom_index)
        picked = blocks[src_glob].astype(jnp.float32)
        product = jnp.einsum("rstij,rstjf->rstif", values[dom_index].astype(jnp.float32), picked)
        product = product * live_mask[..., None, None]
        segment_ids = row_ids[:, None, None] * slot_total + slot_ids[dom_index]
        partial_value = jax.ops.segment_sum(product.reshape(-1, BLOCK, channels), segment_ids.reshape(-1),
                                      num_segments=N_ROWS * slot_total).astype(jnp.bfloat16)
        slot_dest = slot_owner[None, :] * BLK_DEV + targets[dom_index]
        summed = jax.ops.segment_sum(partial_value.astype(jnp.float32), slot_dest.reshape(-1),
                                     num_segments=N_ROWS * BLK_DEV)
        return summed.astype(jnp.bfloat16)

    aggregate = lax.map(forward_dom, jnp.arange(N_DOM, dtype=jnp.int32)).reshape(-1, channels)
    pre_act = jnp.dot(aggregate, weight, preferred_element_type=jnp.float32)
    activations = jax.nn.silu(pre_act).astype(jnp.bfloat16)
    sigmoid_pre = jax.nn.sigmoid(pre_act)
    slope_factor = sigmoid_pre * (1.0 + pre_act * (1.0 - sigmoid_pre))
    pre_grad = (cotangent.astype(jnp.float32) * slope_factor).astype(jnp.bfloat16)
    weight_grad = jnp.dot(aggregate.T, pre_grad, preferred_element_type=jnp.float32)
    agg_grad = jnp.dot(pre_grad, weight.T, preferred_element_type=jnp.float32).astype(jnp.bfloat16)
    grad_blocks = agg_grad.reshape(-1, BLOCK, channels)

    def backward_dom(source_grad, dom_index):
        src_glob, live_mask, dest_local = layout(dom_index)
        picked = grad_blocks[dom_index * N_ROWS * BLK_DEV + dest_local].astype(jnp.float32)
        product = jnp.einsum("rstji,rstjf->rstif", values[dom_index].astype(jnp.float32), picked)
        product = product * live_mask[..., None, None]
        source_grad = source_grad.at[src_glob.reshape(-1)].add(product.reshape(-1, BLOCK, channels))
        return source_grad, None

    start_grad = jnp.zeros((blocks.shape[0], BLOCK, channels), jnp.float32)
    source_grad = lax.scan(backward_dom, start_grad, jnp.arange(N_DOM, dtype=jnp.int32))[0]
    feature_grad = source_grad.reshape(-1, channels).astype(jnp.bfloat16)
    return activations, feature_grad, weight_grad
```

```python
import functools

import jax
import jax.numpy as jnp
from jax import lax
from jax.experimental import pallas as pl
from jax.experimental.pallas import tpu as pltpu
from jax.sharding import PartitionSpec as P

MESH = pl.DeviceIdType.MESH
B = 128
LANES = 128
OWN, NEAR, FAR, MATE, PASSED = range(5)
f32 = jnp.float32
bf16 = jnp.bfloat16


def dot(a, b):
    return jnp.dot(a, b, preferred_element_type=f32)


def kernel(
    dom_count, row_count,
    feat_ref, weight_ref, tiles_ref, source_ref, slot_ref, block_ref, count_ref, cot_ref,
    act_out, grad_out, wg_out,
    tiles, weight, weight_t, cot, sums, sums_t, picked, acc,
    own0, near0, far0, mate0, passed0, own1, near1, far1, mate1, passed1,
    ids_send, ids_recv,
    part_send, part_recv, agg, pre, pre_grad, agg_grad,
    reply_send, back0, back1,
    g_own, g_send, g_recv,
    wg_local, wg_rows, wg_chunk, wg_dom, wg_own,
    load_sem, feat_ss, feat_rs, ids_ss, ids_rs, part_ss, part_rs, reply_ss, reply_rs,
    g_ss, g_rs, w1_ss, w1_rs, w2_ss, w2_rs, w3_ss, w3_rs, w4_ss, w4_rs, out_sem,
):
    d = lax.axis_index("dom")
    r = lax.axis_index("rows")
    parity = d % 2
    sigma = 1 - 2 * parity
    halves = feat_ref.shape[1] // LANES
    nblk = feat_ref.shape[0] // B
    tps = tiles_ref.shape[2]
    cap = block_ref.shape[1] // row_count
    nodes = nblk * B
    mate_dev = (d + sigma, r)
    up_dev = (lax.rem(d + 2 * sigma + dom_count, dom_count), r)
    down_dev = (lax.rem(d - 2 * sigma + dom_count, dom_count), r)
    steps = (2, 2 + 2 * sigma, 2 - 2 * sigma, 2 + sigma, 2 - sigma)
    feats = ((own0, near0, far0, mate0, passed0), (own1, near1, far1, mate1, passed1))
    backs = (back0, back1)

    def row_at(shift):
        return lax.rem(r + shift + row_count, row_count)

    def dom_at(shift):
        return lax.rem(d + shift + dom_count, dom_count)

    def remote(src, dst, ss, rs, device):
        return pltpu.make_async_remote_copy(
            src_ref=src, dst_ref=dst, send_sem=ss, recv_sem=rs, device_id=device, device_id_type=MESH
        )

    barrier = pltpu.get_barrier_semaphore()

    @pl.loop(1, dom_count)
    def _(j):
        pl.semaphore_signal(barrier, inc=1, device_id=(dom_at(j), r), device_id_type=MESH)

    @pl.loop(1, row_count)
    def _(j):
        pl.semaphore_signal(barrier, inc=1, device_id=(d, row_at(j)), device_id_type=MESH)

    loads = [
        pltpu.make_async_copy(tiles_ref.at[0], tiles, load_sem.at[0]),
        pltpu.make_async_copy(weight_ref, weight, load_sem.at[1]),
        pltpu.make_async_copy(cot_ref, cot, load_sem.at[2]),
    ]
    for h in range(halves):
        for b in range(nblk):
            loads.append(
                pltpu.make_async_copy(
                    feat_ref.at[pl.ds(b * B, B), pl.ds(h * LANES, LANES)],
                    feats[h][OWN].at[b],
                    load_sem.at[3 + h * nblk + b],
                )
            )
    for copy in loads:
        copy.start()
    for copy in loads[3:]:
        copy.wait()
    pl.semaphore_wait(barrier, dom_count + row_count - 2)

    def feat_copy(h, role):
        own = feats[h][OWN]
        if role == PASSED:
            src, device = feats[h][NEAR], mate_dev
        elif role == MATE:
            src, device = own, mate_dev
        elif role == FAR:
            src, device = own, up_dev
        else:
            src, device = own, down_dev
        return remote(src, feats[h][role], feat_ss.at[h, role], feat_rs.at[h, role], device)

    for h in range(halves):
        for role in (NEAR, FAR, MATE):
            feat_copy(h, role).start()

    @pl.loop(0, row_count)
    def _(q):
        for c in range(cap):
            ids_send[q, c] = jnp.full((8, LANES), block_ref[0, q * cap + c], jnp.int32)

    ids_recv[0] = ids_send[r]

    def ids_copy(j):
        return remote(ids_send.at[row_at(j)], ids_recv.at[j], ids_ss.at[j], ids_rs.at[j], (d, row_at(j)))

    @pl.loop(1, row_count)
    def _(j):
        ids_copy(j).start()

    for copy in loads[:3]:
        copy.wait()

    def live(role, t):
        return t < count_ref[0, steps[role]]

    @pl.loop(0, row_count)
    def _(q):
        for role in range(5):
            for c in range(cap):
                for t in range(tps):
                    hit = live(role, t) & (slot_ref[0, steps[role], t] == q * cap + c)
                    scale = jnp.where(hit, 1.0, 0.0).astype(f32)
                    tile = tiles[steps[role], t].astype(f32) * scale
                    sums[role, pl.ds(pl.multiple_of((q * cap + c) * B, B), B), t * B:(t + 1) * B] = tile.astype(bf16)

    for role in range(5):
        for t in range(tps):
            turned = tiles[steps[role], t].astype(f32).T
            for b in range(nblk):
                hit = live(role, t) & (source_ref[0, steps[role], t] == b)
                scale = jnp.where(hit, 1.0, 0.0).astype(f32)
                sums_t[role, b * B:(b + 1) * B, t * B:(t + 1) * B] = (turned * scale).astype(bf16)
    weight_t[...] = weight[...].astype(f32).T.astype(bf16)

    total = row_count * cap * B
    span = min(total, 1024)

    def add_role(h, role, first):
        for t in range(tps):
            index = jnp.where(live(role, t), source_ref[0, steps[role], t], 0)
            picked[t * B:(t + 1) * B, :] = feats[h][role][index]

        @pl.loop(0, total // span)
        def _(i):
            rows = pl.ds(pl.multiple_of(i * span, span), span)
            product = dot(sums[role, rows, :], picked[...])
            if first:
                acc[rows, :] = product
            else:
                acc[rows, :] += product

    def part_copy(h, j):
        return remote(
            part_send.at[h, row_at(j)], part_recv.at[h, j], part_ss.at[h, j], part_rs.at[h, j], (d, row_at(j))
        )

    for h in range(halves):
        add_role(h, OWN, True)
        feat_copy(h, NEAR).wait_recv()
        feat_copy(h, PASSED).start()
        feat_copy(h, MATE).wait_recv()
        add_role(h, MATE, False)
        add_role(h, NEAR, False)
        feat_copy(h, FAR).wait_recv()
        add_role(h, FAR, False)
        feat_copy(h, PASSED).wait_recv()
        add_role(h, PASSED, False)

        @pl.loop(0, row_count)
        def _(q):
            rows = pl.ds(pl.multiple_of(q * cap * B, cap * B), cap * B)
            part_send[h, q] = acc[rows, :].astype(bf16)

        @pl.loop(1, row_count)
        def _(j):
            part_copy(h, j).start()

        part_recv[h, 0] = part_send[h, r]

    @pl.loop(1, row_count)
    def _(j):
        ids_copy(j).wait()

    def is_block(j, c, b):
        return ids_recv[j, c][0:1, :] == b

    for h in range(halves):
        @pl.loop(1, row_count)
        def _(j):
            part_copy(h, j).wait_recv()

        for b in range(nblk):
            def gather(j, value):
                for c in range(cap):
                    term = part_recv[h, j, c * B:(c + 1) * B, :].astype(f32)
                    value = value + jnp.where(is_block(j, c, b), term, 0.0)
                return value

            value = lax.fori_loop(0, row_count, gather, jnp.zeros((B, LANES), f32), unroll=row_count <= 4)
            agg[h, b * B:(b + 1) * B, :] = value.astype(bf16)
        product = dot(agg[h], weight[h * LANES:(h + 1) * LANES, :])
        if h == 0:
            pre[...] = product
        else:
            pre[...] += product

    value = pre[...]
    sig = jax.nn.sigmoid(value)
    slope = sig * (1.0 + value * (1.0 - sig))
    pre_grad[...] = (cot[...].astype(f32) * slope).astype(bf16)

    def reply_copy(h, j):
        rows = pl.ds(pl.multiple_of(r * cap, cap), cap)
        return remote(
            reply_send.at[h, j], backs[h].at[rows], reply_ss.at[h, j], reply_rs.at[h, j], (d, row_at(-j))
        )

    for h in range(halves):
        product = dot(pre_grad[...], weight_t[:, h * LANES:(h + 1) * LANES])
        agg_grad[...] = product.astype(bf16)

        @pl.loop(0, row_count)
        def _(j):
            for c in range(cap):
                chosen = jnp.zeros((B, LANES), f32)
                for b in range(nblk):
                    chosen = jnp.where(is_block(j, c, b), agg_grad[b * B:(b + 1) * B, :].astype(f32), chosen)
                reply_send[h, j, c] = chosen.astype(bf16)

        @pl.loop(1, row_count)
        def _(j):
            reply_copy(h, j).start()

        backs[h][pl.ds(pl.multiple_of(r * cap, cap), cap)] = reply_send[h, 0]

    act_out[...] = (value * sig).astype(bf16)

    for h in range(halves):
        wg_local[h * LANES:(h + 1) * LANES, :] = lax.dot_general(
            agg[h], pre_grad[...], (((0,), (0,)), ((), ())), preferred_element_type=f32
        )
    chunk = wg_local.shape[0] // row_count

    def w1_copy(j):
        rows = pl.ds(pl.multiple_of(row_at(j) * chunk, chunk), chunk)
        return remote(wg_local.at[rows], wg_rows.at[j], w1_ss.at[j], w1_rs.at[j], (d, row_at(j)))

    @pl.loop(1, row_count)
    def _(j):
        w1_copy(j).start()

    def g_copy(h, role):
        device = {NEAR: up_dev, FAR: down_dev, MATE: mate_dev, PASSED: mate_dev}[role]
        return remote(g_send.at[h, role], g_recv.at[h, role], g_ss.at[h, role], g_rs.at[h, role], device)

    for h in range(halves):
        @pl.loop(1, row_count)
        def _(j):
            reply_copy(h, j).wait_recv()

        def source_terms(role):
            for t in range(tps):
                index = jnp.where(live(role, t), slot_ref[0, steps[role], t], 0)
                picked[t * B:(t + 1) * B, :] = backs[h][index]
            return dot(sums_t[role], picked[...])

        for role in (PASSED, FAR):
            g_send[h, role] = source_terms(role).astype(bf16)
            g_copy(h, role).start()
        near = source_terms(NEAR)
        g_copy(h, PASSED).wait_recv()
        g_send[h, NEAR] = (near + g_recv[h, PASSED].astype(f32)).astype(bf16)
        g_copy(h, NEAR).start()
        g_send[h, MATE] = source_terms(MATE).astype(bf16)
        g_copy(h, MATE).start()
        g_own[h] = source_terms(OWN)

    wg_chunk[...] = wg_local[pl.ds(pl.multiple_of(r * chunk, chunk), chunk), :]

    @pl.loop(1, row_count)
    def _(j):
        w1_copy(j).wait_recv()
        wg_chunk[...] += wg_rows[j]

    piece = chunk // dom_count
    scatter = piece * dom_count == chunk and piece % 8 == 0
    mine = pl.ds(pl.multiple_of(r * chunk, chunk), chunk)
    if scatter:
        def w2_copy(j):
            rows = pl.ds(pl.multiple_of(dom_at(j) * piece, piece), piece)
            return remote(wg_chunk.at[rows], wg_dom.at[j], w2_ss.at[j], w2_rs.at[j], (dom_at(j), r))

        @pl.loop(1, dom_count)
        def _(j):
            w2_copy(j).start()

        wg_own[...] = wg_chunk[pl.ds(pl.multiple_of(d * piece, piece), piece), :]

        @pl.loop(1, dom_count)
        def _(j):
            w2_copy(j).wait_recv()
            wg_own[...] += wg_dom[j]

        def w3_copy(j):
            rows = pl.ds(pl.multiple_of(r * chunk + d * piece, piece), piece)
            return remote(wg_own, wg_out.at[rows], w3_ss.at[j], w3_rs.at[j], (dom_at(j), r))

        @pl.loop(1, dom_count)
        def _(j):
            w3_copy(j).start()

        wg_out[pl.ds(pl.multiple_of(r * chunk + d * piece, piece), piece), :] = wg_own[...]

        @pl.loop(1, dom_count)
        def _(j):
            w3_copy(j).wait()
    else:
        def w2_copy(j):
            return remote(wg_chunk, wg_dom.at[d], w2_ss.at[j], w2_rs.at[j], (dom_at(j), r))

        @pl.loop(1, dom_count)
        def _(j):
            w2_copy(j).start()

        wg_dom[d] = wg_chunk[...]

        @pl.loop(1, dom_count)
        def _(j):
            w2_copy(j).wait_recv()

        wg_out[mine, :] = lax.fori_loop(
            0, dom_count, lambda i, value: value + wg_dom[i], jnp.zeros(wg_chunk.shape, f32)
        )

    def w4_copy(j):
        return remote(wg_out.at[mine], wg_out.at[mine], w4_ss.at[j], w4_rs.at[j], (d, row_at(j)))

    @pl.loop(1, row_count)
    def _(j):
        w4_copy(j).start()

    for h in range(halves):
        for role in (MATE, NEAR, FAR):
            g_copy(h, role).wait_recv()
        value = g_own[h]
        for role in (MATE, NEAR, FAR):
            value = value + g_recv[h, role].astype(f32)
        grad_out[:, h * LANES:(h + 1) * LANES] = value.astype(bf16)

    @pl.loop(1, row_count)
    def _(j):
        w4_copy(j).wait()

    for h in range(halves):
        for role in (NEAR, FAR, MATE, PASSED):
            feat_copy(h, role).wait_send()
            g_copy(h, role).wait_send()

        @pl.loop(1, row_count)
        def _(j):
            part_copy(h, j).wait_send()
            reply_copy(h, j).wait_send()

    @pl.loop(1, row_count)
    def _(j):
        w1_copy(j).wait_send()

    @pl.loop(1, dom_count)
    def _(j):
        w2_copy(j).wait_send()


def per_device(
    features, weight, tile_values, tile_source, tile_slot, slot_block, tile_count, cotangent, *, dom_count, row_count
):
    nodes, channels = features.shape
    nblk = nodes // B
    halves = channels // LANES
    tps = tile_values.shape[2]
    slots = slot_block.shape[1]
    cap = slots // row_count
    chunk = channels // row_count
    piece = chunk // dom_count
    scatter = piece * dom_count == chunk and piece % 8 == 0
    vmem = pl.BlockSpec(memory_space=pltpu.VMEM)
    smem = pl.BlockSpec(memory_space=pltpu.SMEM)
    anywhere = pl.BlockSpec(memory_space=pl.ANY)
    V = pltpu.VMEM
    dma = pltpu.SemaphoreType.DMA
    scratch = [
        V(tile_values.shape[1:], bf16), V(weight.shape, bf16), V(weight.shape[::-1], bf16), V(cotangent.shape, bf16),
        V((5, slots * B, tps * B), bf16), V((5, nodes, tps * B), bf16), V((tps * B, LANES), bf16),
        V((slots * B, LANES), f32),
        *[V((nblk, B, LANES), bf16) for _ in range(10)],
        V((row_count, cap, 8, LANES), jnp.int32), V((row_count, cap, 8, LANES), jnp.int32),
        V((halves, row_count, cap * B, LANES), bf16), V((halves, row_count, cap * B, LANES), bf16),
        V((halves, nodes, LANES), bf16), V((nodes, channels), f32), V((nodes, channels), bf16), V((nodes, LANES), bf16),
        V((halves, row_count, cap, B, LANES), bf16), V((slots, B, LANES), bf16), V((slots, B, LANES), bf16),
        V((halves, nodes, LANES), f32), V((halves, 5, nodes, LANES), bf16), V((halves, 5, nodes, LANES), bf16),
        V((channels, channels), f32), V((row_count, chunk, channels), f32), V((chunk, channels), f32),
        V((dom_count, piece if scatter else chunk, channels), f32), V((piece if scatter else 8, channels), f32),
        dma((3 + halves * nblk,)), dma((halves, 5)), dma((halves, 5)), dma((row_count,)), dma((row_count,)),
        dma((halves, row_count)), dma((halves, row_count)), dma((halves, row_count)), dma((halves, row_count)),
        dma((halves, 5)), dma((halves, 5)),
        dma((row_count,)), dma((row_count,)), dma((dom_count,)), dma((dom_count,)),
        dma((dom_count,)), dma((dom_count,)), dma((row_count,)), dma((row_count,)), dma((1,)),
    ]
    return pl.pallas_call(
        functools.partial(kernel, dom_count, row_count),
        out_shape=(
            jax.ShapeDtypeStruct((nodes, channels), bf16),
            jax.ShapeDtypeStruct((nodes, channels), bf16),
            jax.ShapeDtypeStruct((channels, channels), f32),
        ),
        in_specs=[anywhere, anywhere, anywhere, smem, smem, smem, smem, anywhere],
        out_specs=(vmem, vmem, vmem),
        scratch_shapes=scratch,
        compiler_params=pltpu.CompilerParams(
            collective_id=0, has_side_effects=True, vmem_limit_bytes=56 * 1024 * 1024
        ),
        name="graph_layer",
    )(features, weight, tile_values, tile_source, tile_slot, slot_block, tile_count, cotangent)


def solution(mesh):
    both = P(("dom", "rows"))
    return jax.shard_map(
        functools.partial(per_device, dom_count=mesh.shape["dom"], row_count=mesh.shape["rows"]),
        mesh=mesh,
        in_specs=(both, P(), both, both, both, both, both, both),
        out_specs=(both, both, P()),
        check_vma=False,
    )
```

```python
import functools

import jax
import jax.numpy as jnp
from jax import lax
from jax.experimental import pallas as pl
from jax.experimental.pallas import tpu as pltpu
from jax.sharding import PartitionSpec as P

MESH = pl.DeviceIdType.MESH
B = 128
LANES = 128
OWN, NEAR, FAR, MATE, PASSED = range(5)
f32 = jnp.float32
bf16 = jnp.bfloat16


def dot(a, b):
    return jnp.dot(a, b, preferred_element_type=f32)


def kernel(
    dom_count, row_count,
    feat_ref, weight_ref, tiles_ref, source_ref, slot_ref, block_ref, count_ref, cot_ref,
    act_out, grad_out, wg_out,
    tiles, weight, weight_t, cot, sums, sums_t, picked, acc,
    own0, near0, far0, mate0, passed0, own1, near1, far1, mate1, passed1,
    ids_send, ids_recv,
    part_send, part_recv, agg, pre, pre_grad, agg_grad,
    reply_send, back0, back1,
    g_own, g_send, g_recv,
    wg_local, wg_rows, wg_chunk, wg_dom, wg_mine, act, grad,
    load_sem, feat_ss, feat_rs, ids_ss, ids_rs, part_ss, part_rs, reply_ss, reply_rs,
    g_ss, g_rs, w1_ss, w1_rs, w2_ss, w2_rs, w3_ss, w3_rs, w4_ss, w4_rs, out_sem,
):
    d = lax.axis_index("dom")
    r = lax.axis_index("rows")
    parity = d % 2
    sigma = 1 - 2 * parity
    halves = feat_ref.shape[2] // LANES
    nblk = feat_ref.shape[0]
    tps = tiles_ref.shape[2]
    cap = block_ref.shape[1] // row_count
    nodes = nblk * B
    mate_dev = (d + sigma, r)
    up_dev = (lax.rem(d + 2 * sigma + dom_count, dom_count), r)
    down_dev = (lax.rem(d - 2 * sigma + dom_count, dom_count), r)
    steps = (2, 2 + 2 * sigma, 2 - 2 * sigma, 2 + sigma, 2 - sigma)
    feats = ((own0, near0, far0, mate0, passed0), (own1, near1, far1, mate1, passed1))
    backs = (back0, back1)

    def row_at(shift):
        return lax.rem(r + shift + row_count, row_count)

    def dom_at(shift):
        return lax.rem(d + shift + dom_count, dom_count)

    def remote(src, dst, ss, rs, device):
        return pltpu.make_async_remote_copy(
            src_ref=src, dst_ref=dst, send_sem=ss, recv_sem=rs, device_id=device, device_id_type=MESH
        )

    barrier = pltpu.get_barrier_semaphore()

    @pl.loop(1, dom_count)
    def _(j):
        pl.semaphore_signal(barrier, inc=1, device_id=(dom_at(j), r), device_id_type=MESH)

    @pl.loop(1, row_count)
    def _(j):
        pl.semaphore_signal(barrier, inc=1, device_id=(d, row_at(j)), device_id_type=MESH)

    def columns(h):
        return feat_ref.at[:, :, pl.ds(h * LANES, LANES)]

    loads = [
        pltpu.make_async_copy(tiles_ref.at[0], tiles, load_sem.at[0]),
        pltpu.make_async_copy(weight_ref, weight, load_sem.at[1]),
        pltpu.make_async_copy(cot_ref, cot, load_sem.at[2]),
    ]
    for h in range(halves):
        loads.append(pltpu.make_async_copy(columns(h), feats[h][OWN], load_sem.at[3 + h]))
    for copy in loads:
        copy.start()
    pl.semaphore_wait(barrier, dom_count + row_count - 2)

    def feat_copy(h, role):
        own = columns(h)
        if role == PASSED:
            src, device = feats[h][NEAR], mate_dev
        elif role == MATE:
            src, device = own, mate_dev
        elif role == FAR:
            src, device = own, up_dev
        else:
            src, device = own, down_dev
        return remote(src, feats[h][role], feat_ss.at[h, role], feat_rs.at[h, role], device)

    for h in range(halves):
        for role in (NEAR, FAR, MATE):
            feat_copy(h, role).start()

    @pl.loop(0, row_count)
    def _(q):
        for c in range(cap):
            ids_send[q, c] = jnp.full((8, LANES), block_ref[0, q * cap + c], jnp.int32)

    ids_recv[0] = ids_send[r]

    def ids_copy(j):
        return remote(ids_send.at[row_at(j)], ids_recv.at[j], ids_ss.at[j], ids_rs.at[j], (d, row_at(j)))

    @pl.loop(1, row_count)
    def _(j):
        ids_copy(j).start()

    for copy in loads:
        copy.wait()

    def live(role, t):
        return t < count_ref[0, steps[role]]

    @pl.loop(0, row_count)
    def _(q):
        for role in range(5):
            for c in range(cap):
                for t in range(tps):
                    hit = live(role, t) & (slot_ref[0, t, steps[role]] == q * cap + c)
                    scale = jnp.where(hit, 1.0, 0.0).astype(f32)
                    tile = tiles[steps[role], t].astype(f32) * scale
                    sums[role, pl.ds(pl.multiple_of((q * cap + c) * B, B), B), t * B:(t + 1) * B] = tile.astype(bf16)

    for role in range(5):
        for t in range(tps):
            turned = tiles[steps[role], t].astype(f32).T
            for b in range(nblk):
                hit = live(role, t) & (source_ref[0, t, steps[role]] == b)
                scale = jnp.where(hit, 1.0, 0.0).astype(f32)
                sums_t[role, b * B:(b + 1) * B, t * B:(t + 1) * B] = (turned * scale).astype(bf16)
    weight_t[...] = weight[...].astype(f32).T.astype(bf16)

    total = row_count * cap * B
    span = min(total, 1024)

    def pick(h, role):
        for t in range(tps):
            index = jnp.where(live(role, t), source_ref[0, t, steps[role]], 0)
            picked[t * B:(t + 1) * B, :] = feats[h][role][index]

    def add_role(h, role, first):
        pick(h, role)

        @pl.loop(0, total // span)
        def _(i):
            rows = pl.ds(pl.multiple_of(i * span, span), span)
            product = dot(sums[role, rows, :], picked[...])
            if first:
                acc[rows, :] = product
            else:
                acc[rows, :] += product

    def part_copy(h, j):
        return remote(
            part_send.at[h, row_at(j)], part_recv.at[h, j], part_ss.at[h, j], part_rs.at[h, j], (d, row_at(j))
        )

    for h in range(halves):
        add_role(h, OWN, True)
        feat_copy(h, NEAR).wait_recv()
        feat_copy(h, PASSED).start()
        feat_copy(h, MATE).wait_recv()
        add_role(h, MATE, False)
        add_role(h, NEAR, False)
        feat_copy(h, FAR).wait_recv()
        add_role(h, FAR, False)
        feat_copy(h, PASSED).wait_recv()
        pick(h, PASSED)

        def finish(q):
            rows = pl.ds(pl.multiple_of(q * cap * B, cap * B), cap * B)
            part_send[h, q] = (acc[rows, :] + dot(sums[PASSED, rows, :], picked[...])).astype(bf16)

        @pl.loop(1, row_count)
        def _(j):
            finish(row_at(j))
            part_copy(h, j).start()

        finish(r)
        part_recv[h, 0] = part_send[h, r]

    @pl.loop(1, row_count)
    def _(j):
        ids_copy(j).wait()

    def is_block(j, c, b):
        return ids_recv[j, c][0:1, :] == b

    for h in range(halves):
        @pl.loop(1, row_count)
        def _(j):
            part_copy(h, j).wait_recv()

        for b in range(nblk):
            def gather(j, value):
                for c in range(cap):
                    term = part_recv[h, j, c * B:(c + 1) * B, :].astype(f32)
                    value = value + jnp.where(is_block(j, c, b), term, 0.0)
                return value

            value = lax.fori_loop(0, row_count, gather, jnp.zeros((B, LANES), f32), unroll=row_count <= 4)
            agg[h, b * B:(b + 1) * B, :] = value.astype(bf16)
        product = dot(agg[h], weight[h * LANES:(h + 1) * LANES, :])
        if h == 0:
            pre[...] = product
        else:
            pre[...] += product

    value = pre[...]
    sig = jax.nn.sigmoid(value)
    slope = sig * (1.0 + value * (1.0 - sig))
    pre_grad[...] = (cot[...].astype(f32) * slope).astype(bf16)

    def reply_copy(h, j):
        rows = pl.ds(pl.multiple_of(r * cap, cap), cap)
        return remote(
            reply_send.at[h, j], backs[h].at[rows], reply_ss.at[h, j], reply_rs.at[h, j], (d, row_at(-j))
        )

    for h in range(halves):
        product = dot(pre_grad[...], weight_t[:, h * LANES:(h + 1) * LANES])
        agg_grad[...] = product.astype(bf16)

        def reply(j):
            for c in range(cap):
                chosen = jnp.zeros((B, LANES), f32)
                for b in range(nblk):
                    chosen = jnp.where(is_block(j, c, b), agg_grad[b * B:(b + 1) * B, :].astype(f32), chosen)
                reply_send[h, j, c] = chosen.astype(bf16)

        @pl.loop(1, row_count)
        def _(j):
            reply(j)
            reply_copy(h, j).start()

        reply(0)
        backs[h][pl.ds(pl.multiple_of(r * cap, cap), cap)] = reply_send[h, 0]

    act[...] = (value * sig).astype(bf16)
    act_copy = pltpu.make_async_copy(act, act_out, out_sem.at[0])
    act_copy.start()

    for h in range(halves):
        wg_local[h * LANES:(h + 1) * LANES, :] = lax.dot_general(
            agg[h], pre_grad[...], (((0,), (0,)), ((), ())), preferred_element_type=f32
        )
    chunk = wg_local.shape[0] // row_count

    def w1_copy(j):
        rows = pl.ds(pl.multiple_of(row_at(j) * chunk, chunk), chunk)
        return remote(wg_local.at[rows], wg_rows.at[j], w1_ss.at[j], w1_rs.at[j], (d, row_at(j)))

    @pl.loop(1, row_count)
    def _(j):
        w1_copy(j).start()

    piece = chunk // dom_count
    scatter = piece * dom_count == chunk and piece % 8 == 0
    part = pl.ds(pl.multiple_of(d * piece, piece), piece)

    def w2_copy(j):
        if scatter:
            rows = pl.ds(pl.multiple_of(dom_at(j) * piece, piece), piece)
            return remote(wg_chunk.at[rows], wg_dom.at[j], w2_ss.at[j], w2_rs.at[j], (dom_at(j), r))
        return remote(wg_chunk, wg_dom.at[d], w2_ss.at[j], w2_rs.at[j], (dom_at(j), r))

    def w3_copy(j):
        return remote(wg_mine.at[part], wg_mine.at[part], w3_ss.at[j], w3_rs.at[j], (dom_at(j), r))

    def w4_copy(j):
        rows = wg_out.at[pl.ds(pl.multiple_of(r * chunk, chunk), chunk)]
        return remote(wg_mine, rows, w4_ss.at[j], w4_rs.at[j], (d, row_at(j)))

    wg_copy = pltpu.make_async_copy(
        wg_mine, wg_out.at[pl.ds(pl.multiple_of(r * chunk, chunk), chunk)], out_sem.at[1 + halves]
    )

    def wg_second():
        wg_chunk[...] = wg_local[pl.ds(pl.multiple_of(r * chunk, chunk), chunk), :]

        @pl.loop(1, row_count)
        def _(j):
            w1_copy(j).wait_recv()
            wg_chunk[...] += wg_rows[j]

        @pl.loop(1, dom_count)
        def _(j):
            w2_copy(j).start()

    def g_copy(h, role):
        device = {NEAR: up_dev, FAR: down_dev, MATE: mate_dev, PASSED: mate_dev}[role]
        return remote(g_send.at[h, role], g_recv.at[h, role], g_ss.at[h, role], g_rs.at[h, role], device)

    for h in range(halves):
        @pl.loop(1, row_count)
        def _(j):
            reply_copy(h, j).wait_recv()

        def source_terms(role):
            for t in range(tps):
                index = jnp.where(live(role, t), slot_ref[0, t, steps[role]], 0)
                picked[t * B:(t + 1) * B, :] = backs[h][index]
            return dot(sums_t[role], picked[...])

        for role in (PASSED, FAR):
            g_send[h, role] = source_terms(role).astype(bf16)
            g_copy(h, role).start()
        near = source_terms(NEAR)
        g_copy(h, PASSED).wait_recv()
        g_send[h, NEAR] = (near + g_recv[h, PASSED].astype(f32)).astype(bf16)
        g_copy(h, NEAR).start()
        g_send[h, MATE] = source_terms(MATE).astype(bf16)
        g_copy(h, MATE).start()
        g_own[h] = source_terms(OWN)
        if h == 0:
            wg_second()

    if scatter:
        total_own = wg_chunk[part, :]
        for j in range(1, dom_count):
            w2_copy(j).wait_recv()
            total_own = total_own + wg_dom[j]
        wg_mine[part, :] = total_own

        @pl.loop(1, dom_count)
        def _(j):
            w3_copy(j).start()

        @pl.loop(1, dom_count)
        def _(j):
            w3_copy(j).wait()
    else:
        wg_dom[d] = wg_chunk[...]

        @pl.loop(1, dom_count)
        def _(j):
            w2_copy(j).wait_recv()

        wg_mine[...] = lax.fori_loop(
            0, dom_count, lambda i, value: value + wg_dom[i], jnp.zeros(wg_chunk.shape, f32)
        )

    @pl.loop(1, row_count)
    def _(j):
        w4_copy(j).start()

    wg_copy.start()

    def grad_copy(h):
        return pltpu.make_async_copy(grad.at[h], grad_out.at[:, pl.ds(h * LANES, LANES)], out_sem.at[1 + h])

    for h in range(halves):
        for role in (MATE, NEAR, FAR):
            g_copy(h, role).wait_recv()
        value = g_own[h]
        for role in (MATE, NEAR, FAR):
            value = value + g_recv[h, role].astype(f32)
        grad[h] = value.astype(bf16)
        grad_copy(h).start()

    @pl.loop(1, row_count)
    def _(j):
        w4_copy(j).wait()

    act_copy.wait()
    wg_copy.wait()
    for h in range(halves):
        for role in (NEAR, FAR, MATE, PASSED):
            feat_copy(h, role).wait_send()
            g_copy(h, role).wait_send()
        grad_copy(h).wait()

        @pl.loop(1, row_count)
        def _(j):
            part_copy(h, j).wait_send()
            reply_copy(h, j).wait_send()

    @pl.loop(1, row_count)
    def _(j):
        w1_copy(j).wait_send()

    @pl.loop(1, dom_count)
    def _(j):
        w2_copy(j).wait_send()


def hand_over(a, b, c, to_a, to_b, to_c, sem):
    copies = [pltpu.make_async_copy(x, y, sem.at[i]) for i, (x, y) in enumerate(((a, to_a), (b, to_b), (c, to_c)))]
    for copy in copies:
        copy.start()
    for copy in copies:
        copy.wait()


def per_device(
    features, weight, tile_values, tile_source, tile_slot, slot_block, tile_count, cotangent, *, dom_count, row_count
):
    nodes, channels = features.shape
    nblk = nodes // B
    halves = channels // LANES
    tps = tile_values.shape[2]
    slots = slot_block.shape[1]
    cap = slots // row_count
    chunk = channels // row_count
    piece = chunk // dom_count
    scatter = piece * dom_count == chunk and piece % 8 == 0
    smem = pl.BlockSpec(memory_space=pltpu.SMEM)
    anywhere = pl.BlockSpec(memory_space=pl.ANY)
    V = pltpu.VMEM
    dma = pltpu.SemaphoreType.DMA
    scratch = [
        V(tile_values.shape[1:], bf16), V(weight.shape, bf16), V(weight.shape[::-1], bf16), V(cotangent.shape, bf16),
        V((5, slots * B, tps * B), bf16), V((5, nodes, tps * B), bf16), V((tps * B, LANES), bf16),
        V((slots * B, LANES), f32),
        *[V((nblk, B, LANES), bf16) for _ in range(10)],
        V((row_count, cap, 8, LANES), jnp.int32), V((row_count, cap, 8, LANES), jnp.int32),
        V((halves, row_count, cap * B, LANES), bf16), V((halves, row_count, cap * B, LANES), bf16),
        V((halves, nodes, LANES), bf16), V((nodes, channels), f32), V((nodes, channels), bf16), V((nodes, LANES), bf16),
        V((halves, row_count, cap, B, LANES), bf16), V((slots, B, LANES), bf16), V((slots, B, LANES), bf16),
        V((halves, nodes, LANES), f32), V((halves, 5, nodes, LANES), bf16), V((halves, 5, nodes, LANES), bf16),
        V((channels, channels), f32), V((row_count, chunk, channels), f32), V((chunk, channels), f32),
        V((dom_count, piece if scatter else chunk, channels), f32), V((chunk, channels), f32),
        V((nodes, channels), bf16), V((halves, nodes, LANES), bf16),
        dma((3 + halves,)), dma((halves, 5)), dma((halves, 5)), dma((row_count,)), dma((row_count,)),
        dma((halves, row_count)), dma((halves, row_count)), dma((halves, row_count)), dma((halves, row_count)),
        dma((halves, 5)), dma((halves, 5)),
        dma((row_count,)), dma((row_count,)), dma((dom_count,)), dma((dom_count,)),
        dma((dom_count,)), dma((dom_count,)), dma((row_count,)), dma((row_count,)), dma((2 + halves,)),
    ]
    results = pl.pallas_call(
        functools.partial(kernel, dom_count, row_count),
        out_shape=(
            jax.ShapeDtypeStruct((nodes, channels), bf16),
            jax.ShapeDtypeStruct((nodes, channels), bf16),
            jax.ShapeDtypeStruct((channels, channels), f32),
        ),
        in_specs=[anywhere, anywhere, anywhere, smem, smem, smem, smem, anywhere],
        out_specs=(anywhere, anywhere, anywhere),
        scratch_shapes=scratch,
        compiler_params=pltpu.CompilerParams(
            collective_id=0, has_side_effects=True, vmem_limit_bytes=56 * 1024 * 1024
        ),
        name="graph_layer",
    )(
        features.reshape(nblk, B, channels), weight, tile_values,
        jnp.swapaxes(tile_source, 1, 2), jnp.swapaxes(tile_slot, 1, 2), slot_block, tile_count, cotangent,
    )
    return pl.pallas_call(
        hand_over,
        out_shape=tuple(jax.ShapeDtypeStruct(x.shape, x.dtype) for x in results),
        in_specs=[anywhere] * 3,
        out_specs=(anywhere,) * 3,
        scratch_shapes=[dma((3,))],
        compiler_params=pltpu.CompilerParams(vmem_limit_bytes=60 * 1024 * 1024),
        name="hand_over",
    )(*results)


def solution(mesh):
    both = P(("dom", "rows"))
    return jax.shard_map(
        functools.partial(per_device, dom_count=mesh.shape["dom"], row_count=mesh.shape["rows"]),
        mesh=mesh,
        in_specs=(both, P(), both, both, both, both, both, both),
        out_specs=(both, both, P()),
        check_vma=False,
    )
```

```python
import functools

import jax
import jax.numpy as jnp
from jax import lax
from jax.experimental import pallas as pl
from jax.experimental.pallas import tpu as pltpu
from jax.sharding import PartitionSpec as P

MESH = pl.DeviceIdType.MESH
B = 128
LANES = 128
OWN, NEAR, FAR, MATE, PASSED = range(5)
f32 = jnp.float32
bf16 = jnp.bfloat16


def dot(a, b):
    return jnp.dot(a, b, preferred_element_type=f32)


def kernel(
    dom_count, row_count,
    feat_ref, weight_ref, tiles_ref, source_ref, slot_ref, block_ref, count_ref, cot_ref,
    act_out, grad_out, wg_out,
    tiles, weight, weight_t, cot, sums, sums_t, picked, acc,
    own0, near0, far0, mate0, passed0, own1, near1, far1, mate1, passed1,
    ids_send, ids_recv,
    part_send, part_recv, agg, pre, pre_grad, agg_grad,
    reply_send, back0, back1,
    g_own, g_send, g_recv,
    wg_local, wg_rows, wg_chunk, wg_dom, wg_mine, act, grad,
    load_sem, feat_ss, feat_rs, ids_ss, ids_rs, part_ss, part_rs, reply_ss, reply_rs,
    g_ss, g_rs, w1_ss, w1_rs, w2_ss, w2_rs, w3_ss, w3_rs, w4_ss, w4_rs, out_sem,
):
    d = lax.axis_index("dom")
    r = lax.axis_index("rows")
    parity = d % 2
    sigma = 1 - 2 * parity
    halves = feat_ref.shape[2] // LANES
    nblk = feat_ref.shape[0]
    tps = tiles_ref.shape[2]
    cap = block_ref.shape[1] // row_count
    nodes = nblk * B
    mate_dev = (d + sigma, r)
    up_dev = (lax.rem(d + 2 * sigma + dom_count, dom_count), r)
    down_dev = (lax.rem(d - 2 * sigma + dom_count, dom_count), r)
    steps = (2, 2 + 2 * sigma, 2 - 2 * sigma, 2 + sigma, 2 - sigma)
    feats = ((own0, near0, far0, mate0, passed0), (own1, near1, far1, mate1, passed1))
    backs = (back0, back1)

    def row_at(shift):
        return lax.rem(r + shift + row_count, row_count)

    def dom_at(shift):
        return lax.rem(d + shift + dom_count, dom_count)

    def remote(src, dst, ss, rs, device):
        return pltpu.make_async_remote_copy(
            src_ref=src, dst_ref=dst, send_sem=ss, recv_sem=rs, device_id=device, device_id_type=MESH
        )

    barrier = pltpu.get_barrier_semaphore()

    @pl.loop(1, dom_count)
    def _(j):
        pl.semaphore_signal(barrier, inc=1, device_id=(dom_at(j), r), device_id_type=MESH)

    @pl.loop(1, row_count)
    def _(j):
        pl.semaphore_signal(barrier, inc=1, device_id=(d, row_at(j)), device_id_type=MESH)

    def columns(h):
        return feat_ref.at[:, :, pl.ds(h * LANES, LANES)]

    loads = [
        pltpu.make_async_copy(tiles_ref.at[0], tiles, load_sem.at[0]),
        pltpu.make_async_copy(weight_ref, weight, load_sem.at[1]),
        pltpu.make_async_copy(cot_ref, cot, load_sem.at[2]),
    ]
    for h in range(halves):
        loads.append(pltpu.make_async_copy(columns(h), feats[h][OWN], load_sem.at[3 + h]))
    for copy in loads:
        copy.start()
    pl.semaphore_wait(barrier, dom_count + row_count - 2)

    def feat_copy(h, role):
        own = columns(h)
        if role == PASSED:
            src, device = feats[h][NEAR], mate_dev
        elif role == MATE:
            src, device = own, mate_dev
        elif role == FAR:
            src, device = own, up_dev
        else:
            src, device = own, down_dev
        return remote(src, feats[h][role], feat_ss.at[h, role], feat_rs.at[h, role], device)

    for h in range(halves):
        for role in (NEAR, FAR, MATE):
            feat_copy(h, role).start()

    @pl.loop(0, row_count)
    def _(q):
        for c in range(cap):
            ids_send[q, c] = jnp.full((8, LANES), block_ref[0, q * cap + c], jnp.int32)

    ids_recv[0] = ids_send[r]

    def ids_copy(j):
        return remote(ids_send.at[row_at(j)], ids_recv.at[j], ids_ss.at[j], ids_rs.at[j], (d, row_at(j)))

    @pl.loop(1, row_count)
    def _(j):
        ids_copy(j).start()

    for copy in loads:
        copy.wait()

    def live(role, t):
        return t < count_ref[0, steps[role]]

    @pl.loop(0, row_count)
    def _(q):
        for role in range(5):
            for c in range(cap):
                for t in range(tps):
                    hit = live(role, t) & (slot_ref[0, t, steps[role]] == q * cap + c)
                    scale = jnp.where(hit, 1.0, 0.0).astype(f32)
                    tile = tiles[steps[role], t].astype(f32) * scale
                    sums[role, pl.ds(pl.multiple_of((q * cap + c) * B, B), B), t * B:(t + 1) * B] = tile.astype(bf16)

    for role in range(5):
        for t in range(tps):
            turned = tiles[steps[role], t].astype(f32).T
            for b in range(nblk):
                hit = live(role, t) & (source_ref[0, t, steps[role]] == b)
                scale = jnp.where(hit, 1.0, 0.0).astype(f32)
                sums_t[role, b * B:(b + 1) * B, t * B:(t + 1) * B] = (turned * scale).astype(bf16)
    weight_t[...] = weight[...].astype(f32).T.astype(bf16)

    total = row_count * cap * B
    span = min(total, 1024)

    def pick(h, role):
        for t in range(tps):
            index = jnp.where(live(role, t), source_ref[0, t, steps[role]], 0)
            picked[t * B:(t + 1) * B, :] = feats[h][role][index]

    def add_role(h, role, first):
        pick(h, role)

        @pl.loop(0, total // span)
        def _(i):
            rows = pl.ds(pl.multiple_of(i * span, span), span)
            product = dot(sums[role, rows, :], picked[...])
            if first:
                acc[rows, :] = product
            else:
                acc[rows, :] += product

    def part_copy(h, j):
        return remote(
            part_send.at[h, row_at(j)], part_recv.at[h, j], part_ss.at[h, j], part_rs.at[h, j], (d, row_at(j))
        )

    for h in range(halves):
        add_role(h, OWN, True)
        feat_copy(h, NEAR).wait_recv()
        feat_copy(h, PASSED).start()
        feat_copy(h, MATE).wait_recv()
        add_role(h, MATE, False)
        add_role(h, NEAR, False)
        feat_copy(h, FAR).wait_recv()
        add_role(h, FAR, False)
        feat_copy(h, PASSED).wait_recv()
        pick(h, PASSED)

        def finish(q):
            rows = pl.ds(pl.multiple_of(q * cap * B, cap * B), cap * B)
            part_send[h, q] = (acc[rows, :] + dot(sums[PASSED, rows, :], picked[...])).astype(bf16)

        @pl.loop(1, row_count)
        def _(j):
            finish(row_at(j))
            part_copy(h, j).start()

        finish(r)
        part_recv[h, 0] = part_send[h, r]

    @pl.loop(1, row_count)
    def _(j):
        ids_copy(j).wait()

    def is_block(j, c, b):
        return ids_recv[j, c][0:1, :] == b

    for h in range(halves):
        @pl.loop(1, row_count)
        def _(j):
            part_copy(h, j).wait_recv()

        for b in range(nblk):
            def gather(j, value):
                for c in range(cap):
                    term = part_recv[h, j, c * B:(c + 1) * B, :].astype(f32)
                    value = value + jnp.where(is_block(j, c, b), term, 0.0)
                return value

            value = lax.fori_loop(0, row_count, gather, jnp.zeros((B, LANES), f32), unroll=row_count <= 4)
            agg[h, b * B:(b + 1) * B, :] = value.astype(bf16)
        product = dot(agg[h], weight[h * LANES:(h + 1) * LANES, :])
        if h == 0:
            pre[...] = product
        else:
            pre[...] += product

    value = pre[...]
    sig = jax.nn.sigmoid(value)
    slope = sig * (1.0 + value * (1.0 - sig))
    pre_grad[...] = (cot[...].astype(f32) * slope).astype(bf16)

    def reply_copy(h, j):
        rows = pl.ds(pl.multiple_of(r * cap, cap), cap)
        return remote(
            reply_send.at[h, j], backs[h].at[rows], reply_ss.at[h, j], reply_rs.at[h, j], (d, row_at(-j))
        )

    for h in range(halves):
        product = dot(pre_grad[...], weight_t[:, h * LANES:(h + 1) * LANES])
        agg_grad[...] = product.astype(bf16)

        def reply(j):
            for c in range(cap):
                chosen = jnp.zeros((B, LANES), f32)
                for b in range(nblk):
                    chosen = jnp.where(is_block(j, c, b), agg_grad[b * B:(b + 1) * B, :].astype(f32), chosen)
                reply_send[h, j, c] = chosen.astype(bf16)

        @pl.loop(1, row_count)
        def _(j):
            reply(j)
            reply_copy(h, j).start()

        reply(0)
        backs[h][pl.ds(pl.multiple_of(r * cap, cap), cap)] = reply_send[h, 0]

    act[...] = (value * sig).astype(bf16)
    act_copy = pltpu.make_async_copy(act, act_out, out_sem.at[0])
    act_copy.start()

    for h in range(halves):
        wg_local[h * LANES:(h + 1) * LANES, :] = lax.dot_general(
            agg[h], pre_grad[...], (((0,), (0,)), ((), ())), preferred_element_type=f32
        )
    chunk = wg_local.shape[0] // row_count

    def w1_copy(j):
        rows = pl.ds(pl.multiple_of(row_at(j) * chunk, chunk), chunk)
        return remote(wg_local.at[rows], wg_rows.at[j], w1_ss.at[j], w1_rs.at[j], (d, row_at(j)))

    @pl.loop(1, row_count)
    def _(j):
        w1_copy(j).start()

    piece = chunk // dom_count
    scatter = piece * dom_count == chunk and piece % 8 == 0
    part = pl.ds(pl.multiple_of(d * piece, piece), piece)

    def w2_copy(j):
        if scatter:
            rows = pl.ds(pl.multiple_of(dom_at(j) * piece, piece), piece)
            return remote(wg_chunk.at[rows], wg_dom.at[j], w2_ss.at[j], w2_rs.at[j], (dom_at(j), r))
        return remote(wg_chunk, wg_dom.at[d], w2_ss.at[j], w2_rs.at[j], (dom_at(j), r))

    def w3_copy(j):
        return remote(wg_mine.at[part], wg_mine.at[part], w3_ss.at[j], w3_rs.at[j], (dom_at(j), r))

    def w4_copy(i, j):
        span = piece if scatter else chunk
        start = dom_at(-i) * piece if scatter else 0
        src = wg_mine.at[pl.ds(pl.multiple_of(start, span), span)]
        dst = wg_out.at[pl.ds(pl.multiple_of(r * chunk + start, span), span)]
        return remote(src, dst, w4_ss.at[i, j], w4_rs.at[i, j], (d, row_at(j)))

    def w4_start(i):
        @pl.loop(1, row_count)
        def _(j):
            w4_copy(i, j).start()

    wg_copy = pltpu.make_async_copy(
        wg_mine, wg_out.at[pl.ds(pl.multiple_of(r * chunk, chunk), chunk)], out_sem.at[1 + halves]
    )

    def wg_second():
        wg_chunk[...] = wg_local[pl.ds(pl.multiple_of(r * chunk, chunk), chunk), :]

        @pl.loop(1, row_count)
        def _(j):
            w1_copy(j).wait_recv()
            wg_chunk[...] += wg_rows[j]

        @pl.loop(1, dom_count)
        def _(j):
            w2_copy(j).start()

    def g_copy(h, role):
        device = {NEAR: up_dev, FAR: down_dev, MATE: mate_dev, PASSED: mate_dev}[role]
        return remote(g_send.at[h, role], g_recv.at[h, role], g_ss.at[h, role], g_rs.at[h, role], device)

    for h in range(halves):
        @pl.loop(1, row_count)
        def _(j):
            reply_copy(h, j).wait_recv()

        def source_terms(role):
            for t in range(tps):
                index = jnp.where(live(role, t), slot_ref[0, t, steps[role]], 0)
                picked[t * B:(t + 1) * B, :] = backs[h][index]
            return dot(sums_t[role], picked[...])

        for role in (PASSED, FAR):
            g_send[h, role] = source_terms(role).astype(bf16)
            g_copy(h, role).start()
        near = source_terms(NEAR)
        g_copy(h, PASSED).wait_recv()
        g_send[h, NEAR] = (near + g_recv[h, PASSED].astype(f32)).astype(bf16)
        g_copy(h, NEAR).start()
        g_send[h, MATE] = source_terms(MATE).astype(bf16)
        g_copy(h, MATE).start()
        g_own[h] = source_terms(OWN)
        if h == 0:
            wg_second()

    if scatter:
        total_own = wg_chunk[part, :]
        for j in range(1, dom_count):
            w2_copy(j).wait_recv()
            total_own = total_own + wg_dom[j]
        wg_mine[part, :] = total_own

        @pl.loop(1, dom_count)
        def _(j):
            w3_copy(j).start()

        w4_start(0)

        @pl.loop(1, dom_count)
        def _(j):
            w3_copy(j).wait_recv()
            w4_start(j)

        @pl.loop(1, dom_count)
        def _(j):
            w3_copy(j).wait_send()
    else:
        wg_dom[d] = wg_chunk[...]

        @pl.loop(1, dom_count)
        def _(j):
            w2_copy(j).wait_recv()

        wg_mine[...] = lax.fori_loop(
            0, dom_count, lambda i, value: value + wg_dom[i], jnp.zeros(wg_chunk.shape, f32)
        )

        w4_start(0)

    wg_copy.start()

    def grad_copy(h):
        return pltpu.make_async_copy(grad.at[h], grad_out.at[:, pl.ds(h * LANES, LANES)], out_sem.at[1 + h])

    for h in range(halves):
        for role in (MATE, NEAR, FAR):
            g_copy(h, role).wait_recv()
        value = g_own[h]
        for role in (MATE, NEAR, FAR):
            value = value + g_recv[h, role].astype(f32)
        grad[h] = value.astype(bf16)
        grad_copy(h).start()

    @pl.loop(0, dom_count if scatter else 1)
    def _(i):
        @pl.loop(1, row_count)
        def _(j):
            w4_copy(i, j).wait()

    act_copy.wait()
    wg_copy.wait()
    for h in range(halves):
        for role in (NEAR, FAR, MATE, PASSED):
            feat_copy(h, role).wait_send()
            g_copy(h, role).wait_send()
        grad_copy(h).wait()

        @pl.loop(1, row_count)
        def _(j):
            part_copy(h, j).wait_send()
            reply_copy(h, j).wait_send()

    @pl.loop(1, row_count)
    def _(j):
        w1_copy(j).wait_send()

    @pl.loop(1, dom_count)
    def _(j):
        w2_copy(j).wait_send()


def hand_over(a, b, c, to_a, to_b, to_c, in_a, in_b, in_c, sem):
    triples = ((a, in_a, to_a), (b, in_b, to_b), (c, in_c, to_c))
    reads = [pltpu.make_async_copy(x, y, sem.at[0, i]) for i, (x, y, _) in enumerate(triples)]
    writes = [pltpu.make_async_copy(y, z, sem.at[1, i]) for i, (_, y, z) in enumerate(triples)]
    for copy in reads:
        copy.start()
    for read, write in zip(reads, writes):
        read.wait()
        write.start()
    for copy in writes:
        copy.wait()


def per_device(
    features, weight, tile_values, tile_source, tile_slot, slot_block, tile_count, cotangent, *, dom_count, row_count
):
    nodes, channels = features.shape
    nblk = nodes // B
    halves = channels // LANES
    tps = tile_values.shape[2]
    slots = slot_block.shape[1]
    cap = slots // row_count
    chunk = channels // row_count
    piece = chunk // dom_count
    scatter = piece * dom_count == chunk and piece % 8 == 0
    smem = pl.BlockSpec(memory_space=pltpu.SMEM)
    anywhere = pl.BlockSpec(memory_space=pl.ANY)
    V = pltpu.VMEM
    dma = pltpu.SemaphoreType.DMA
    scratch = [
        V(tile_values.shape[1:], bf16), V(weight.shape, bf16), V(weight.shape[::-1], bf16), V(cotangent.shape, bf16),
        V((5, slots * B, tps * B), bf16), V((5, nodes, tps * B), bf16), V((tps * B, LANES), bf16),
        V((slots * B, LANES), f32),
        *[V((nblk, B, LANES), bf16) for _ in range(10)],
        V((row_count, cap, 8, LANES), jnp.int32), V((row_count, cap, 8, LANES), jnp.int32),
        V((halves, row_count, cap * B, LANES), bf16), V((halves, row_count, cap * B, LANES), bf16),
        V((halves, nodes, LANES), bf16), V((nodes, channels), f32), V((nodes, channels), bf16), V((nodes, LANES), bf16),
        V((halves, row_count, cap, B, LANES), bf16), V((slots, B, LANES), bf16), V((slots, B, LANES), bf16),
        V((halves, nodes, LANES), f32), V((halves, 5, nodes, LANES), bf16), V((halves, 5, nodes, LANES), bf16),
        V((channels, channels), f32), V((row_count, chunk, channels), f32), V((chunk, channels), f32),
        V((dom_count, piece if scatter else chunk, channels), f32), V((chunk, channels), f32),
        V((nodes, channels), bf16), V((halves, nodes, LANES), bf16),
        dma((3 + halves,)), dma((halves, 5)), dma((halves, 5)), dma((row_count,)), dma((row_count,)),
        dma((halves, row_count)), dma((halves, row_count)), dma((halves, row_count)), dma((halves, row_count)),
        dma((halves, 5)), dma((halves, 5)),
        dma((row_count,)), dma((row_count,)), dma((dom_count,)), dma((dom_count,)),
        dma((dom_count,)), dma((dom_count,)), dma((dom_count, row_count)), dma((dom_count, row_count)), dma((2 + halves,)),
    ]
    results = pl.pallas_call(
        functools.partial(kernel, dom_count, row_count),
        out_shape=(
            jax.ShapeDtypeStruct((nodes, channels), bf16),
            jax.ShapeDtypeStruct((nodes, channels), bf16),
            jax.ShapeDtypeStruct((channels, channels), f32),
        ),
        in_specs=[anywhere, anywhere, anywhere, smem, smem, smem, smem, anywhere],
        out_specs=(anywhere, anywhere, anywhere),
        scratch_shapes=scratch,
        compiler_params=pltpu.CompilerParams(
            collective_id=0, has_side_effects=True, vmem_limit_bytes=56 * 1024 * 1024
        ),
        name="graph_layer",
    )(
        features.reshape(nblk, B, channels), weight, tile_values,
        jnp.swapaxes(tile_source, 1, 2), jnp.swapaxes(tile_slot, 1, 2), slot_block, tile_count, cotangent,
    )
    return pl.pallas_call(
        hand_over,
        out_shape=tuple(jax.ShapeDtypeStruct(x.shape, x.dtype) for x in results),
        in_specs=[anywhere] * 3,
        out_specs=(anywhere,) * 3,
        scratch_shapes=[*[V(x.shape, x.dtype) for x in results], dma((2, 3))],
        compiler_params=pltpu.CompilerParams(vmem_limit_bytes=60 * 1024 * 1024),
        name="hand_over",
    )(*results)


def solution(mesh):
    both = P(("dom", "rows"))
    return jax.shard_map(
        functools.partial(per_device, dom_count=mesh.shape["dom"], row_count=mesh.shape["rows"]),
        mesh=mesh,
        in_specs=(both, P(), both, both, both, both, both, both),
        out_specs=(both, both, P()),
        check_vma=False,
    )
```

```python
import functools

import jax
import jax.numpy as jnp
from jax import lax
from jax.experimental import pallas as pl
from jax.experimental.pallas import tpu as pltpu
from jax.sharding import PartitionSpec as P

MESH = pl.DeviceIdType.MESH
B = 128
LANES = 128
OWN, NEAR, FAR, MATE, PASSED = range(5)
f32 = jnp.float32
bf16 = jnp.bfloat16


def dot(a, b):
    return jnp.dot(a, b, preferred_element_type=f32)


def kernel(
    dom_count, row_count,
    feat_ref, weight_ref, tiles_ref, source_ref, slot_ref, block_ref, count_ref, cot_ref,
    act_out, grad_out, wg_out,
    tiles, weight, weight_t, cot, sums, sums_t, picked, acc,
    own0, near0, far0, mate0, passed0, own1, near1, far1, mate1, passed1,
    ids_send, ids_recv,
    part_send, part_recv, agg, pre, pre_grad, agg_grad,
    reply_send, back0, back1,
    g_own, g_send, g_recv,
    wg_local, wg_rows, wg_chunk, wg_dom, wg_mine, act, grad,
    load_sem, feat_ss, feat_rs, ids_ss, ids_rs, part_ss, part_rs, reply_ss, reply_rs,
    g_ss, g_rs, w1_ss, w1_rs, w2_ss, w2_rs, w3_ss, w3_rs, w4_ss, w4_rs, out_sem,
):
    d = lax.axis_index("dom")
    r = lax.axis_index("rows")
    parity = d % 2
    sigma = 1 - 2 * parity
    halves = feat_ref.shape[2] // LANES
    nblk = feat_ref.shape[0]
    tps = tiles_ref.shape[2]
    cap = block_ref.shape[1] // row_count
    nodes = nblk * B
    mate_dev = (d + sigma, r)
    up_dev = (lax.rem(d + 2 * sigma + dom_count, dom_count), r)
    down_dev = (lax.rem(d - 2 * sigma + dom_count, dom_count), r)
    steps = (2, 2 + 2 * sigma, 2 - 2 * sigma, 2 + sigma, 2 - sigma)
    feats = ((own0, near0, far0, mate0, passed0), (own1, near1, far1, mate1, passed1))
    backs = (back0, back1)

    def row_at(shift):
        return lax.rem(r + shift + row_count, row_count)

    def dom_at(shift):
        return lax.rem(d + shift + dom_count, dom_count)

    def remote(src, dst, ss, rs, device):
        return pltpu.make_async_remote_copy(
            src_ref=src, dst_ref=dst, send_sem=ss, recv_sem=rs, device_id=device, device_id_type=MESH
        )

    barrier = pltpu.get_barrier_semaphore()

    @pl.loop(1, dom_count)
    def _(j):
        pl.semaphore_signal(barrier, inc=1, device_id=(dom_at(j), r), device_id_type=MESH)

    @pl.loop(1, row_count)
    def _(j):
        pl.semaphore_signal(barrier, inc=1, device_id=(d, row_at(j)), device_id_type=MESH)

    def columns(h):
        return feat_ref.at[:, :, pl.ds(h * LANES, LANES)]

    loads = [
        pltpu.make_async_copy(tiles_ref.at[0], tiles, load_sem.at[0]),
        pltpu.make_async_copy(weight_ref, weight, load_sem.at[1]),
        pltpu.make_async_copy(cot_ref, cot, load_sem.at[2]),
    ]
    for h in range(halves):
        loads.append(pltpu.make_async_copy(columns(h), feats[h][OWN], load_sem.at[3 + h]))
    for copy in loads:
        copy.start()
    pl.semaphore_wait(barrier, dom_count + row_count - 2)

    def feat_copy(h, role):
        own = columns(h)
        if role == PASSED:
            src, device = feats[h][NEAR], mate_dev
        elif role == MATE:
            src, device = own, mate_dev
        elif role == FAR:
            src, device = own, up_dev
        else:
            src, device = own, down_dev
        return remote(src, feats[h][role], feat_ss.at[h, role], feat_rs.at[h, role], device)

    for role in (NEAR, FAR, MATE):
        feat_copy(0, role).start()

    @pl.loop(0, row_count)
    def _(q):
        for c in range(cap):
            ids_send[q, c] = jnp.full((8, LANES), block_ref[0, q * cap + c], jnp.int32)

    ids_recv[0] = ids_send[r]

    def ids_copy(j):
        return remote(ids_send.at[row_at(j)], ids_recv.at[j], ids_ss.at[j], ids_rs.at[j], (d, row_at(j)))

    @pl.loop(1, row_count)
    def _(j):
        ids_copy(j).start()

    for copy in loads:
        copy.wait()

    def live(role, t):
        return t < count_ref[0, steps[role]]

    @pl.loop(0, row_count)
    def _(q):
        for role in range(5):
            for c in range(cap):
                for t in range(tps):
                    hit = live(role, t) & (slot_ref[0, t, steps[role]] == q * cap + c)
                    scale = jnp.where(hit, 1.0, 0.0).astype(f32)
                    tile = tiles[steps[role], t].astype(f32) * scale
                    sums[role, pl.ds(pl.multiple_of((q * cap + c) * B, B), B), t * B:(t + 1) * B] = tile.astype(bf16)

    for role in range(5):
        for t in range(tps):
            turned = tiles[steps[role], t].astype(f32).T
            for b in range(nblk):
                hit = live(role, t) & (source_ref[0, t, steps[role]] == b)
                scale = jnp.where(hit, 1.0, 0.0).astype(f32)
                sums_t[role, b * B:(b + 1) * B, t * B:(t + 1) * B] = (turned * scale).astype(bf16)
    weight_t[...] = weight[...].astype(f32).T.astype(bf16)

    for h in range(1, halves):
        for role in (NEAR, FAR):
            feat_copy(h - 1, role).wait_send()
        for role in (NEAR, FAR, MATE):
            feat_copy(h, role).start()

    total = row_count * cap * B
    span = min(total, 1024)

    def pick(h, role):
        for t in range(tps):
            index = jnp.where(live(role, t), source_ref[0, t, steps[role]], 0)
            picked[t * B:(t + 1) * B, :] = feats[h][role][index]

    def add_role(h, role, first):
        pick(h, role)

        @pl.loop(0, total // span)
        def _(i):
            rows = pl.ds(pl.multiple_of(i * span, span), span)
            product = dot(sums[role, rows, :], picked[...])
            if first:
                acc[rows, :] = product
            else:
                acc[rows, :] += product

    def part_copy(h, j):
        return remote(
            part_send.at[h, row_at(j)], part_recv.at[h, j], part_ss.at[h, j], part_rs.at[h, j], (d, row_at(j))
        )

    for h in range(halves):
        add_role(h, OWN, True)
        feat_copy(h, NEAR).wait_recv()
        feat_copy(h, PASSED).start()
        feat_copy(h, MATE).wait_recv()
        add_role(h, MATE, False)
        add_role(h, NEAR, False)
        feat_copy(h, FAR).wait_recv()
        add_role(h, FAR, False)
        feat_copy(h, PASSED).wait_recv()
        pick(h, PASSED)

        def finish(q):
            rows = pl.ds(pl.multiple_of(q * cap * B, cap * B), cap * B)
            part_send[h, q] = (acc[rows, :] + dot(sums[PASSED, rows, :], picked[...])).astype(bf16)

        @pl.loop(1, row_count)
        def _(j):
            finish(row_at(j))
            part_copy(h, j).start()

        finish(r)
        part_recv[h, 0] = part_send[h, r]

    @pl.loop(1, row_count)
    def _(j):
        ids_copy(j).wait()

    def is_block(j, c, b):
        return ids_recv[j, c][0:1, :] == b

    for h in range(halves):
        @pl.loop(1, row_count)
        def _(j):
            part_copy(h, j).wait_recv()

        for b in range(nblk):
            def gather(j, value):
                for c in range(cap):
                    term = part_recv[h, j, c * B:(c + 1) * B, :].astype(f32)
                    value = value + jnp.where(is_block(j, c, b), term, 0.0)
                return value

            value = lax.fori_loop(0, row_count, gather, jnp.zeros((B, LANES), f32), unroll=row_count <= 4)
            agg[h, b * B:(b + 1) * B, :] = value.astype(bf16)
        product = dot(agg[h], weight[h * LANES:(h + 1) * LANES, :])
        if h == 0:
            pre[...] = product
        else:
            pre[...] += product

    value = pre[...]
    sig = jax.nn.sigmoid(value)
    slope = sig * (1.0 + value * (1.0 - sig))
    pre_grad[...] = (cot[...].astype(f32) * slope).astype(bf16)

    def reply_copy(h, j):
        rows = pl.ds(pl.multiple_of(r * cap, cap), cap)
        return remote(
            reply_send.at[h, j], backs[h].at[rows], reply_ss.at[h, j], reply_rs.at[h, j], (d, row_at(-j))
        )

    for h in range(halves):
        product = dot(pre_grad[...], weight_t[:, h * LANES:(h + 1) * LANES])
        agg_grad[...] = product.astype(bf16)

        def reply(j):
            for c in range(cap):
                chosen = jnp.zeros((B, LANES), f32)
                for b in range(nblk):
                    chosen = jnp.where(is_block(j, c, b), agg_grad[b * B:(b + 1) * B, :].astype(f32), chosen)
                reply_send[h, j, c] = chosen.astype(bf16)

        @pl.loop(1, row_count)
        def _(j):
            reply(j)
            reply_copy(h, j).start()

        reply(0)
        backs[h][pl.ds(pl.multiple_of(r * cap, cap), cap)] = reply_send[h, 0]

    act[...] = (value * sig).astype(bf16)
    act_copy = pltpu.make_async_copy(act, act_out, out_sem.at[0])
    act_copy.start()

    for h in range(halves):
        wg_local[h * LANES:(h + 1) * LANES, :] = lax.dot_general(
            agg[h], pre_grad[...], (((0,), (0,)), ((), ())), preferred_element_type=f32
        )
    chunk = wg_local.shape[0] // row_count

    def w1_copy(j):
        rows = pl.ds(pl.multiple_of(row_at(j) * chunk, chunk), chunk)
        return remote(wg_local.at[rows], wg_rows.at[j], w1_ss.at[j], w1_rs.at[j], (d, row_at(j)))

    @pl.loop(1, row_count)
    def _(j):
        w1_copy(j).start()

    piece = chunk // dom_count
    scatter = piece * dom_count == chunk and piece % 8 == 0
    part = pl.ds(pl.multiple_of(d * piece, piece), piece)

    def w2_copy(j):
        if scatter:
            rows = pl.ds(pl.multiple_of(dom_at(j) * piece, piece), piece)
            return remote(wg_chunk.at[rows], wg_dom.at[j], w2_ss.at[j], w2_rs.at[j], (dom_at(j), r))
        return remote(wg_chunk, wg_dom.at[d], w2_ss.at[j], w2_rs.at[j], (dom_at(j), r))

    def w3_copy(j):
        return remote(wg_mine.at[part], wg_mine.at[part], w3_ss.at[j], w3_rs.at[j], (dom_at(j), r))

    def w4_copy(i, j):
        span = piece if scatter else chunk
        start = dom_at(-i) * piece if scatter else 0
        src = wg_mine.at[pl.ds(pl.multiple_of(start, span), span)]
        dst = wg_out.at[pl.ds(pl.multiple_of(r * chunk + start, span), span)]
        return remote(src, dst, w4_ss.at[i, j], w4_rs.at[i, j], (d, row_at(j)))

    def w4_start(i):
        @pl.loop(1, row_count)
        def _(j):
            w4_copy(i, j).start()

    wg_copy = pltpu.make_async_copy(
        wg_mine, wg_out.at[pl.ds(pl.multiple_of(r * chunk, chunk), chunk)], out_sem.at[1 + halves]
    )

    def wg_second():
        wg_chunk[...] = wg_local[pl.ds(pl.multiple_of(r * chunk, chunk), chunk), :]

        @pl.loop(1, row_count)
        def _(j):
            w1_copy(j).wait_recv()
            wg_chunk[...] += wg_rows[j]

        @pl.loop(1, dom_count)
        def _(j):
            w2_copy(j).start()

    def g_copy(h, role):
        device = {NEAR: up_dev, FAR: down_dev, MATE: mate_dev, PASSED: mate_dev}[role]
        return remote(g_send.at[h, role], g_recv.at[h, role], g_ss.at[h, role], g_rs.at[h, role], device)

    for h in range(halves):
        @pl.loop(1, row_count)
        def _(j):
            reply_copy(h, j).wait_recv()

        def source_terms(role):
            for t in range(tps):
                index = jnp.where(live(role, t), slot_ref[0, t, steps[role]], 0)
                picked[t * B:(t + 1) * B, :] = backs[h][index]
            return dot(sums_t[role], picked[...])

        for role in (PASSED, FAR):
            g_send[h, role] = source_terms(role).astype(bf16)
            g_copy(h, role).start()
        near = source_terms(NEAR)
        g_copy(h, PASSED).wait_recv()
        g_send[h, NEAR] = (near + g_recv[h, PASSED].astype(f32)).astype(bf16)
        g_copy(h, NEAR).start()
        g_send[h, MATE] = source_terms(MATE).astype(bf16)
        g_copy(h, MATE).start()
        g_own[h] = source_terms(OWN)
        if h == 0:
            wg_second()

    if scatter:
        total_own = wg_chunk[part, :]
        for j in range(1, dom_count):
            w2_copy(j).wait_recv()
            total_own = total_own + wg_dom[j]
        wg_mine[part, :] = total_own

        @pl.loop(1, dom_count)
        def _(j):
            w3_copy(j).start()

        w4_start(0)

        @pl.loop(1, dom_count)
        def _(j):
            w3_copy(j).wait_recv()
            w4_start(j)

        @pl.loop(1, dom_count)
        def _(j):
            w3_copy(j).wait_send()
    else:
        wg_dom[d] = wg_chunk[...]

        @pl.loop(1, dom_count)
        def _(j):
            w2_copy(j).wait_recv()

        wg_mine[...] = lax.fori_loop(
            0, dom_count, lambda i, value: value + wg_dom[i], jnp.zeros(wg_chunk.shape, f32)
        )

        w4_start(0)

    wg_copy.start()

    def grad_copy(h):
        return pltpu.make_async_copy(grad.at[h], grad_out.at[:, pl.ds(h * LANES, LANES)], out_sem.at[1 + h])

    for h in range(halves):
        for role in (MATE, NEAR, FAR):
            g_copy(h, role).wait_recv()
        value = g_own[h]
        for role in (MATE, NEAR, FAR):
            value = value + g_recv[h, role].astype(f32)
        grad[h] = value.astype(bf16)
        grad_copy(h).start()

    @pl.loop(0, dom_count if scatter else 1)
    def _(i):
        @pl.loop(1, row_count)
        def _(j):
            w4_copy(i, j).wait()

    act_copy.wait()
    wg_copy.wait()
    for h in range(halves):
        for role in (NEAR, FAR, MATE, PASSED):
            if h == halves - 1 or role in (MATE, PASSED):
                feat_copy(h, role).wait_send()
            g_copy(h, role).wait_send()
        grad_copy(h).wait()

        @pl.loop(1, row_count)
        def _(j):
            part_copy(h, j).wait_send()
            reply_copy(h, j).wait_send()

    @pl.loop(1, row_count)
    def _(j):
        w1_copy(j).wait_send()

    @pl.loop(1, dom_count)
    def _(j):
        w2_copy(j).wait_send()


def hand_over(a, b, c, to_a, to_b, to_c, in_a, in_b, in_c, sem):
    triples = ((a, in_a, to_a), (b, in_b, to_b), (c, in_c, to_c))
    reads = [pltpu.make_async_copy(x, y, sem.at[0, i]) for i, (x, y, _) in enumerate(triples)]
    writes = [pltpu.make_async_copy(y, z, sem.at[1, i]) for i, (_, y, z) in enumerate(triples)]
    for copy in reads:
        copy.start()
    for read, write in zip(reads, writes):
        read.wait()
        write.start()
    for copy in writes:
        copy.wait()


def per_device(
    features, weight, tile_values, tile_source, tile_slot, slot_block, tile_count, cotangent, *, dom_count, row_count
):
    nodes, channels = features.shape
    nblk = nodes // B
    halves = channels // LANES
    tps = tile_values.shape[2]
    slots = slot_block.shape[1]
    cap = slots // row_count
    chunk = channels // row_count
    piece = chunk // dom_count
    scatter = piece * dom_count == chunk and piece % 8 == 0
    smem = pl.BlockSpec(memory_space=pltpu.SMEM)
    anywhere = pl.BlockSpec(memory_space=pl.ANY)
    V = pltpu.VMEM
    dma = pltpu.SemaphoreType.DMA
    scratch = [
        V(tile_values.shape[1:], bf16), V(weight.shape, bf16), V(weight.shape[::-1], bf16), V(cotangent.shape, bf16),
        V((5, slots * B, tps * B), bf16), V((5, nodes, tps * B), bf16), V((tps * B, LANES), bf16),
        V((slots * B, LANES), f32),
        *[V((nblk, B, LANES), bf16) for _ in range(10)],
        V((row_count, cap, 8, LANES), jnp.int32), V((row_count, cap, 8, LANES), jnp.int32),
        V((halves, row_count, cap * B, LANES), bf16), V((halves, row_count, cap * B, LANES), bf16),
        V((halves, nodes, LANES), bf16), V((nodes, channels), f32), V((nodes, channels), bf16), V((nodes, LANES), bf16),
        V((halves, row_count, cap, B, LANES), bf16), V((slots, B, LANES), bf16), V((slots, B, LANES), bf16),
        V((halves, nodes, LANES), f32), V((halves, 5, nodes, LANES), bf16), V((halves, 5, nodes, LANES), bf16),
        V((channels, channels), f32), V((row_count, chunk, channels), f32), V((chunk, channels), f32),
        V((dom_count, piece if scatter else chunk, channels), f32), V((chunk, channels), f32),
        V((nodes, channels), bf16), V((halves, nodes, LANES), bf16),
        dma((3 + halves,)), dma((halves, 5)), dma((halves, 5)), dma((row_count,)), dma((row_count,)),
        dma((halves, row_count)), dma((halves, row_count)), dma((halves, row_count)), dma((halves, row_count)),
        dma((halves, 5)), dma((halves, 5)),
        dma((row_count,)), dma((row_count,)), dma((dom_count,)), dma((dom_count,)),
        dma((dom_count,)), dma((dom_count,)), dma((dom_count, row_count)), dma((dom_count, row_count)), dma((2 + halves,)),
    ]
    results = pl.pallas_call(
        functools.partial(kernel, dom_count, row_count),
        out_shape=(
            jax.ShapeDtypeStruct((nodes, channels), bf16),
            jax.ShapeDtypeStruct((nodes, channels), bf16),
            jax.ShapeDtypeStruct((channels, channels), f32),
        ),
        in_specs=[anywhere, anywhere, anywhere, smem, smem, smem, smem, anywhere],
        out_specs=(anywhere, anywhere, anywhere),
        scratch_shapes=scratch,
        compiler_params=pltpu.CompilerParams(
            collective_id=0, has_side_effects=True, vmem_limit_bytes=56 * 1024 * 1024
        ),
        name="graph_layer",
    )(
        features.reshape(nblk, B, channels), weight, tile_values,
        jnp.swapaxes(tile_source, 1, 2), jnp.swapaxes(tile_slot, 1, 2), slot_block, tile_count, cotangent,
    )
    return pl.pallas_call(
        hand_over,
        out_shape=tuple(jax.ShapeDtypeStruct(x.shape, x.dtype) for x in results),
        in_specs=[anywhere] * 3,
        out_specs=(anywhere,) * 3,
        scratch_shapes=[*[V(x.shape, x.dtype) for x in results], dma((2, 3))],
        compiler_params=pltpu.CompilerParams(vmem_limit_bytes=60 * 1024 * 1024),
        name="hand_over",
    )(*results)


def solution(mesh):
    both = P(("dom", "rows"))
    return jax.shard_map(
        functools.partial(per_device, dom_count=mesh.shape["dom"], row_count=mesh.shape["rows"]),
        mesh=mesh,
        in_specs=(both, P(), both, both, both, both, both, both),
        out_specs=(both, both, P()),
        check_vma=False,
    )
```

```python
import functools

import jax
import jax.numpy as jnp
from jax import lax
from jax.experimental import pallas as pl
from jax.experimental.pallas import tpu as pltpu
from jax.sharding import PartitionSpec as P

MESH = pl.DeviceIdType.MESH
B = 128
LANES = 128
OWN, NEAR, FAR, MATE, PASSED = range(5)
f32 = jnp.float32
bf16 = jnp.bfloat16


def dot(a, b):
    return jnp.dot(a, b, preferred_element_type=f32)


def kernel(
    dom_count, row_count,
    feat_ref, weight_ref, tiles_ref, source_ref, slot_ref, block_ref, count_ref, cot_ref,
    act_out, grad_out, wg_out,
    tiles, tiles_t, weight, weight_t, cot, prod, acc,
    own0, near0, far0, mate0, passed0, own1, near1, far1, mate1, passed1,
    ids_send, ids_recv,
    part_send, part_recv, agg, pre, pre_grad, agg_grad,
    reply_send, back0, back1,
    g_own, g_send, g_recv,
    wg_local, wg_rows, wg_chunk, wg_dom, wg_mine, act, grad,
    load_sem, feat_ss, feat_rs, ids_ss, ids_rs, part_ss, part_rs, reply_ss, reply_rs,
    g_ss, g_rs, w1_ss, w1_rs, w2_ss, w2_rs, w3_ss, w3_rs, w4_ss, w4_rs, out_sem,
):
    d = lax.axis_index("dom")
    r = lax.axis_index("rows")
    parity = d % 2
    sigma = 1 - 2 * parity
    halves = feat_ref.shape[2] // LANES
    nblk = feat_ref.shape[0]
    tps = tiles_ref.shape[2]
    cap = block_ref.shape[1] // row_count
    nodes = nblk * B
    mate_dev = (d + sigma, r)
    up_dev = (lax.rem(d + 2 * sigma + dom_count, dom_count), r)
    down_dev = (lax.rem(d - 2 * sigma + dom_count, dom_count), r)
    steps = (2, 2 + 2 * sigma, 2 - 2 * sigma, 2 + sigma, 2 - sigma)
    feats = ((own0, near0, far0, mate0, passed0), (own1, near1, far1, mate1, passed1))
    backs = (back0, back1)

    def row_at(shift):
        return lax.rem(r + shift + row_count, row_count)

    def dom_at(shift):
        return lax.rem(d + shift + dom_count, dom_count)

    def remote(src, dst, ss, rs, device):
        return pltpu.make_async_remote_copy(
            src_ref=src, dst_ref=dst, send_sem=ss, recv_sem=rs, device_id=device, device_id_type=MESH
        )

    barrier = pltpu.get_barrier_semaphore()

    @pl.loop(1, dom_count)
    def _(j):
        pl.semaphore_signal(barrier, inc=1, device_id=(dom_at(j), r), device_id_type=MESH)

    @pl.loop(1, row_count)
    def _(j):
        pl.semaphore_signal(barrier, inc=1, device_id=(d, row_at(j)), device_id_type=MESH)

    def columns(h):
        return feat_ref.at[:, :, pl.ds(h * LANES, LANES)]

    loads = [
        pltpu.make_async_copy(tiles_ref.at[0], tiles, load_sem.at[0]),
        pltpu.make_async_copy(weight_ref, weight, load_sem.at[1]),
        pltpu.make_async_copy(cot_ref, cot, load_sem.at[2]),
    ]
    for h in range(halves):
        loads.append(pltpu.make_async_copy(columns(h), feats[h][OWN], load_sem.at[3 + h]))
    for copy in loads:
        copy.start()
    pl.semaphore_wait(barrier, dom_count + row_count - 2)

    def feat_copy(h, role):
        own = columns(h)
        if role == PASSED:
            src, device = feats[h][NEAR], mate_dev
        elif role == MATE:
            src, device = own, mate_dev
        elif role == FAR:
            src, device = own, up_dev
        else:
            src, device = own, down_dev
        return remote(src, feats[h][role], feat_ss.at[h, role], feat_rs.at[h, role], device)

    for h in range(halves):
        for role in (NEAR, FAR, MATE):
            feat_copy(h, role).start()

    @pl.loop(0, row_count)
    def _(q):
        for c in range(cap):
            ids_send[q, c] = jnp.full((8, LANES), block_ref[0, q * cap + c], jnp.int32)

    ids_recv[0] = ids_send[r]

    def ids_copy(j):
        return remote(ids_send.at[row_at(j)], ids_recv.at[j], ids_ss.at[j], ids_rs.at[j], (d, row_at(j)))

    @pl.loop(1, row_count)
    def _(j):
        ids_copy(j).start()

    for copy in loads:
        copy.wait()

    def live(role, t):
        return t < count_ref[0, steps[role]]

    @pl.loop(0, tiles.shape[0])
    def _(k):
        for t in range(tps):
            tiles_t[k, t] = tiles[k, t].astype(f32).T.astype(bf16)

    weight_t[...] = weight[...].astype(f32).T.astype(bf16)

    def products(matrices, blocks, index_ref, role):
        for t in range(tps):
            index = jnp.where(live(role, t), index_ref[0, t, steps[role]], 0)
            prod[t] = dot(matrices[steps[role], t], blocks[index])

    def mixed(index_ref, role, wanted):
        value = None
        for t in range(tps):
            hit = live(role, t) & (index_ref[0, t, steps[role]] == wanted)
            term = prod[t] * jnp.where(hit, 1.0, 0.0).astype(f32)
            value = term if value is None else value + term
        return value

    def add_role(h, role, first):
        products(tiles, feats[h][role], source_ref, role)

        @pl.loop(0, row_count * cap)
        def _(slot):
            value = mixed(slot_ref, role, slot)
            acc[slot] = value if first else acc[slot] + value

    def part_copy(h, j):
        return remote(
            part_send.at[h, row_at(j)], part_recv.at[h, j], part_ss.at[h, j], part_rs.at[h, j], (d, row_at(j))
        )

    for h in range(halves):
        add_role(h, OWN, True)
        feat_copy(h, NEAR).wait_recv()
        feat_copy(h, PASSED).start()
        feat_copy(h, MATE).wait_recv()
        add_role(h, MATE, False)
        add_role(h, NEAR, False)
        feat_copy(h, FAR).wait_recv()
        add_role(h, FAR, False)
        feat_copy(h, PASSED).wait_recv()
        products(tiles, feats[h][PASSED], source_ref, PASSED)

        def finish(q):
            for c in range(cap):
                value = acc[q * cap + c] + mixed(slot_ref, PASSED, q * cap + c)
                part_send[h, q, c * B:(c + 1) * B, :] = value.astype(bf16)

        @pl.loop(1, row_count)
        def _(j):
            finish(row_at(j))
            part_copy(h, j).start()

        finish(r)
        part_recv[h, 0] = part_send[h, r]

    @pl.loop(1, row_count)
    def _(j):
        ids_copy(j).wait()

    def is_block(j, c, b):
        return ids_recv[j, c][0:1, :] == b

    for h in range(halves):
        @pl.loop(1, row_count)
        def _(j):
            part_copy(h, j).wait_recv()

        @pl.loop(0, nblk)
        def _(b):
            def gather(j, value):
                for c in range(cap):
                    term = part_recv[h, j, c * B:(c + 1) * B, :].astype(f32)
                    value = value + jnp.where(is_block(j, c, b), term, 0.0)
                return value

            value = lax.fori_loop(0, row_count, gather, jnp.zeros((B, LANES), f32), unroll=row_count <= 4)
            rows = pl.ds(pl.multiple_of(b * B, B), B)
            agg[h, rows, :] = value.astype(bf16)
            product = dot(value.astype(bf16), weight[h * LANES:(h + 1) * LANES, :])
            if h > 0:
                product = pre[rows, :] + product
            pre[rows, :] = product
            if h == halves - 1:
                sig = jax.nn.sigmoid(product)
                slope = sig * (1.0 + product * (1.0 - sig))
                pre_grad[rows, :] = (cot[rows, :].astype(f32) * slope).astype(bf16)
                act[rows, :] = (product * sig).astype(bf16)

    act_copy = pltpu.make_async_copy(act, act_out, out_sem.at[0])
    act_copy.start()

    def reply_copy(h, j):
        rows = pl.ds(pl.multiple_of(r * cap, cap), cap)
        return remote(
            reply_send.at[h, j], backs[h].at[rows], reply_ss.at[h, j], reply_rs.at[h, j], (d, row_at(-j))
        )

    for h in range(halves):
        product = dot(pre_grad[...], weight_t[:, h * LANES:(h + 1) * LANES])
        agg_grad[...] = product.astype(bf16)

        def reply(j):
            for c in range(cap):
                chosen = jnp.zeros((B, LANES), f32)
                for b in range(nblk):
                    chosen = jnp.where(is_block(j, c, b), agg_grad[b * B:(b + 1) * B, :].astype(f32), chosen)
                reply_send[h, j, c] = chosen.astype(bf16)

        @pl.loop(1, row_count)
        def _(j):
            reply(j)
            reply_copy(h, j).start()

        reply(0)
        backs[h][pl.ds(pl.multiple_of(r * cap, cap), cap)] = reply_send[h, 0]


    for h in range(halves):
        wg_local[h * LANES:(h + 1) * LANES, :] = lax.dot_general(
            agg[h], pre_grad[...], (((0,), (0,)), ((), ())), preferred_element_type=f32
        )
    chunk = wg_local.shape[0] // row_count

    def w1_copy(j):
        rows = pl.ds(pl.multiple_of(row_at(j) * chunk, chunk), chunk)
        return remote(wg_local.at[rows], wg_rows.at[j], w1_ss.at[j], w1_rs.at[j], (d, row_at(j)))

    @pl.loop(1, row_count)
    def _(j):
        w1_copy(j).start()

    piece = chunk // dom_count
    scatter = piece * dom_count == chunk and piece % 8 == 0
    part = pl.ds(pl.multiple_of(d * piece, piece), piece)

    def w2_copy(j):
        if scatter:
            rows = pl.ds(pl.multiple_of(dom_at(j) * piece, piece), piece)
            return remote(wg_chunk.at[rows], wg_dom.at[j], w2_ss.at[j], w2_rs.at[j], (dom_at(j), r))
        return remote(wg_chunk, wg_dom.at[d], w2_ss.at[j], w2_rs.at[j], (dom_at(j), r))

    def w3_copy(j):
        return remote(wg_mine.at[part], wg_mine.at[part], w3_ss.at[j], w3_rs.at[j], (dom_at(j), r))

    def w4_copy(i, j):
        span = piece if scatter else chunk
        start = dom_at(-i) * piece if scatter else 0
        src = wg_mine.at[pl.ds(pl.multiple_of(start, span), span)]
        dst = wg_out.at[pl.ds(pl.multiple_of(r * chunk + start, span), span)]
        return remote(src, dst, w4_ss.at[i, j], w4_rs.at[i, j], (d, row_at(j)))

    def w4_start(i):
        @pl.loop(1, row_count)
        def _(j):
            w4_copy(i, j).start()

    wg_copy = pltpu.make_async_copy(
        wg_mine, wg_out.at[pl.ds(pl.multiple_of(r * chunk, chunk), chunk)], out_sem.at[1 + halves]
    )

    def wg_second():
        wg_chunk[...] = wg_local[pl.ds(pl.multiple_of(r * chunk, chunk), chunk), :]

        @pl.loop(1, row_count)
        def _(j):
            w1_copy(j).wait_recv()
            wg_chunk[...] += wg_rows[j]

        @pl.loop(1, dom_count)
        def _(j):
            w2_copy(j).start()

    def g_copy(h, role):
        device = {NEAR: up_dev, FAR: down_dev, MATE: mate_dev, PASSED: mate_dev}[role]
        return remote(g_send.at[h, role], g_recv.at[h, role], g_ss.at[h, role], g_rs.at[h, role], device)

    for h in range(halves):
        @pl.loop(1, row_count)
        def _(j):
            reply_copy(h, j).wait_recv()

        def source_terms(role, target, extra=None):
            products(tiles_t, backs[h], slot_ref, role)

            @pl.loop(0, nblk)
            def _(b):
                rows = pl.ds(pl.multiple_of(b * B, B), B)
                value = mixed(source_ref, role, b)
                if extra is not None:
                    value = value + extra[rows, :].astype(f32)
                target[rows, :] = value.astype(target.dtype)

        for role in (PASSED, FAR):
            source_terms(role, g_send.at[h, role])
            g_copy(h, role).start()
        g_copy(h, PASSED).wait_recv()
        source_terms(NEAR, g_send.at[h, NEAR], g_recv.at[h, PASSED])
        g_copy(h, NEAR).start()
        source_terms(MATE, g_send.at[h, MATE])
        g_copy(h, MATE).start()
        source_terms(OWN, g_own.at[h])
        if h == 0:
            wg_second()

    if scatter:
        total_own = wg_chunk[part, :]
        for j in range(1, dom_count):
            w2_copy(j).wait_recv()
            total_own = total_own + wg_dom[j]
        wg_mine[part, :] = total_own

        @pl.loop(1, dom_count)
        def _(j):
            w3_copy(j).start()

        w4_start(0)

        @pl.loop(1, dom_count)
        def _(j):
            w3_copy(j).wait_recv()
            w4_start(j)

        @pl.loop(1, dom_count)
        def _(j):
            w3_copy(j).wait_send()
    else:
        wg_dom[d] = wg_chunk[...]

        @pl.loop(1, dom_count)
        def _(j):
            w2_copy(j).wait_recv()

        wg_mine[...] = lax.fori_loop(
            0, dom_count, lambda i, value: value + wg_dom[i], jnp.zeros(wg_chunk.shape, f32)
        )

        w4_start(0)

    wg_copy.start()

    def grad_copy(h):
        return pltpu.make_async_copy(grad.at[h], grad_out.at[:, pl.ds(h * LANES, LANES)], out_sem.at[1 + h])

    for h in range(halves):
        for role in (MATE, NEAR, FAR):
            g_copy(h, role).wait_recv()
        value = g_own[h]
        for role in (MATE, NEAR, FAR):
            value = value + g_recv[h, role].astype(f32)
        grad[h] = value.astype(bf16)
        grad_copy(h).start()

    @pl.loop(0, dom_count if scatter else 1)
    def _(i):
        @pl.loop(1, row_count)
        def _(j):
            w4_copy(i, j).wait()

    act_copy.wait()
    wg_copy.wait()
    for h in range(halves):
        for role in (NEAR, FAR, MATE, PASSED):
            feat_copy(h, role).wait_send()
            g_copy(h, role).wait_send()
        grad_copy(h).wait()

        @pl.loop(1, row_count)
        def _(j):
            part_copy(h, j).wait_send()
            reply_copy(h, j).wait_send()

    @pl.loop(1, row_count)
    def _(j):
        w1_copy(j).wait_send()

    @pl.loop(1, dom_count)
    def _(j):
        w2_copy(j).wait_send()


def hand_over(a, b, c, to_a, to_b, to_c, in_a, in_b, in_c, sem):
    triples = ((a, in_a, to_a), (b, in_b, to_b), (c, in_c, to_c))
    reads = [pltpu.make_async_copy(x, y, sem.at[0, i]) for i, (x, y, _) in enumerate(triples)]
    writes = [pltpu.make_async_copy(y, z, sem.at[1, i]) for i, (_, y, z) in enumerate(triples)]
    for copy in reads:
        copy.start()
    for read, write in zip(reads, writes):
        read.wait()
        write.start()
    for copy in writes:
        copy.wait()


def per_device(
    features, weight, tile_values, tile_source, tile_slot, slot_block, tile_count, cotangent, *, dom_count, row_count
):
    nodes, channels = features.shape
    nblk = nodes // B
    halves = channels // LANES
    tps = tile_values.shape[2]
    slots = slot_block.shape[1]
    cap = slots // row_count
    chunk = channels // row_count
    piece = chunk // dom_count
    scatter = piece * dom_count == chunk and piece % 8 == 0
    smem = pl.BlockSpec(memory_space=pltpu.SMEM)
    anywhere = pl.BlockSpec(memory_space=pl.ANY)
    V = pltpu.VMEM
    dma = pltpu.SemaphoreType.DMA
    scratch = [
        V(tile_values.shape[1:], bf16), V(tile_values.shape[1:], bf16), V(weight.shape, bf16), V(weight.shape[::-1], bf16), V(cotangent.shape, bf16),
        V((tps, B, LANES), f32), V((slots, B, LANES), f32),
        *[V((nblk, B, LANES), bf16) for _ in range(10)],
        V((row_count, cap, 8, LANES), jnp.int32), V((row_count, cap, 8, LANES), jnp.int32),
        V((halves, row_count, cap * B, LANES), bf16), V((halves, row_count, cap * B, LANES), bf16),
        V((halves, nodes, LANES), bf16), V((nodes, channels), f32), V((nodes, channels), bf16), V((nodes, LANES), bf16),
        V((halves, row_count, cap, B, LANES), bf16), V((slots, B, LANES), bf16), V((slots, B, LANES), bf16),
        V((halves, nodes, LANES), f32), V((halves, 5, nodes, LANES), bf16), V((halves, 5, nodes, LANES), bf16),
        V((channels, channels), f32), V((row_count, chunk, channels), f32), V((chunk, channels), f32),
        V((dom_count, piece if scatter else chunk, channels), f32), V((chunk, channels), f32),
        V((nodes, channels), bf16), V((halves, nodes, LANES), bf16),
        dma((3 + halves,)), dma((halves, 5)), dma((halves, 5)), dma((row_count,)), dma((row_count,)),
        dma((halves, row_count)), dma((halves, row_count)), dma((halves, row_count)), dma((halves, row_count)),
        dma((halves, 5)), dma((halves, 5)),
        dma((row_count,)), dma((row_count,)), dma((dom_count,)), dma((dom_count,)),
        dma((dom_count,)), dma((dom_count,)), dma((dom_count, row_count)), dma((dom_count, row_count)), dma((2 + halves,)),
    ]
    results = pl.pallas_call(
        functools.partial(kernel, dom_count, row_count),
        out_shape=(
            jax.ShapeDtypeStruct((nodes, channels), bf16),
            jax.ShapeDtypeStruct((nodes, channels), bf16),
            jax.ShapeDtypeStruct((channels, channels), f32),
        ),
        in_specs=[anywhere, anywhere, anywhere, smem, smem, smem, smem, anywhere],
        out_specs=(anywhere, anywhere, anywhere),
        scratch_shapes=scratch,
        compiler_params=pltpu.CompilerParams(
            collective_id=0, has_side_effects=True, vmem_limit_bytes=56 * 1024 * 1024
        ),
        name="graph_layer",
    )(
        features.reshape(nblk, B, channels), weight, tile_values,
        jnp.swapaxes(tile_source, 1, 2), jnp.swapaxes(tile_slot, 1, 2), slot_block, tile_count, cotangent,
    )
    return pl.pallas_call(
        hand_over,
        out_shape=tuple(jax.ShapeDtypeStruct(x.shape, x.dtype) for x in results),
        in_specs=[anywhere] * 3,
        out_specs=(anywhere,) * 3,
        scratch_shapes=[*[V(x.shape, x.dtype) for x in results], dma((2, 3))],
        compiler_params=pltpu.CompilerParams(vmem_limit_bytes=60 * 1024 * 1024),
        name="hand_over",
    )(*results)


def solution(mesh):
    both = P(("dom", "rows"))
    return jax.shard_map(
        functools.partial(per_device, dom_count=mesh.shape["dom"], row_count=mesh.shape["rows"]),
        mesh=mesh,
        in_specs=(both, P(), both, both, both, both, both, both),
        out_specs=(both, both, P()),
        check_vma=False,
    )
```

```python
import functools

import jax
import jax.numpy as jnp
from jax import lax
from jax.experimental import pallas as pl
from jax.experimental.pallas import tpu as pltpu
from jax.sharding import PartitionSpec as P

MESH = pl.DeviceIdType.MESH
B = 128
LANES = 128
OWN, NEAR, FAR, MATE, PASSED = range(5)
f32 = jnp.float32
bf16 = jnp.bfloat16


def dot(a, b):
    return jnp.dot(a, b, preferred_element_type=f32)


def kernel(
    dom_count, row_count,
    feat_ref, weight_ref, tiles_ref, source_ref, slot_ref, block_ref, count_ref, cot_ref,
    act_out, grad_out, wg_out,
    tiles, tiles_t, weight, weight_t, cot, prod, acc,
    own0, near0, far0, mate0, passed0, own1, near1, far1, mate1, passed1,
    ids_send, ids_recv,
    part_send, part_recv, agg, pre, pre_grad, agg_grad,
    reply_send, back0, back1,
    g_own, g_send, g_recv,
    wg_local, wg_send, wg_rows, wg_chunk, wg_pieces, wg_dom, wg_mine, wg_all, act, grad,
    load_sem, feat_ss, feat_rs, ids_ss, ids_rs, part_ss, part_rs, reply_ss, reply_rs,
    g_ss, g_rs, w1_ss, w1_rs, w2_ss, w2_rs, w3_ss, w3_rs, w4_ss, w4_rs, out_sem,
):
    d = lax.axis_index("dom")
    r = lax.axis_index("rows")
    parity = d % 2
    sigma = 1 - 2 * parity
    halves = feat_ref.shape[2] // LANES
    nblk = feat_ref.shape[0]
    tps = tiles_ref.shape[2]
    cap = block_ref.shape[1] // row_count
    nodes = nblk * B
    mate_dev = (d + sigma, r)
    up_dev = (lax.rem(d + 2 * sigma + dom_count, dom_count), r)
    down_dev = (lax.rem(d - 2 * sigma + dom_count, dom_count), r)
    steps = (2, 2 + 2 * sigma, 2 - 2 * sigma, 2 + sigma, 2 - sigma)
    feats = ((own0, near0, far0, mate0, passed0), (own1, near1, far1, mate1, passed1))
    backs = (back0, back1)

    def row_at(shift):
        return lax.rem(r + shift + row_count, row_count)

    def dom_at(shift):
        return lax.rem(d + shift + dom_count, dom_count)

    def remote(src, dst, ss, rs, device):
        return pltpu.make_async_remote_copy(
            src_ref=src, dst_ref=dst, send_sem=ss, recv_sem=rs, device_id=device, device_id_type=MESH
        )

    barrier = pltpu.get_barrier_semaphore()

    @pl.loop(1, dom_count)
    def _(j):
        pl.semaphore_signal(barrier, inc=1, device_id=(dom_at(j), r), device_id_type=MESH)

    @pl.loop(1, row_count)
    def _(j):
        pl.semaphore_signal(barrier, inc=1, device_id=(d, row_at(j)), device_id_type=MESH)

    def columns(h):
        return feat_ref.at[:, :, pl.ds(h * LANES, LANES)]

    loads = [
        pltpu.make_async_copy(tiles_ref.at[0], tiles, load_sem.at[0]),
        pltpu.make_async_copy(weight_ref, weight, load_sem.at[1]),
        pltpu.make_async_copy(cot_ref, cot, load_sem.at[2]),
    ]
    for h in range(halves):
        loads.append(pltpu.make_async_copy(columns(h), feats[h][OWN], load_sem.at[3 + h]))
    for copy in loads:
        copy.start()
    pl.semaphore_wait(barrier, dom_count + row_count - 2)

    def feat_copy(h, role):
        own = columns(h)
        if role == PASSED:
            src, device = feats[h][NEAR], mate_dev
        elif role == MATE:
            src, device = own, mate_dev
        elif role == FAR:
            src, device = own, up_dev
        else:
            src, device = own, down_dev
        return remote(src, feats[h][role], feat_ss.at[h, role], feat_rs.at[h, role], device)

    for h in range(halves):
        for role in (NEAR, FAR, MATE):
            feat_copy(h, role).start()

    @pl.loop(0, row_count)
    def _(q):
        for c in range(cap):
            ids_send[q, c] = jnp.full((8, LANES), block_ref[0, q * cap + c], jnp.int32)

    ids_recv[0] = ids_send[r]

    def ids_copy(j):
        return remote(ids_send.at[row_at(j)], ids_recv.at[j], ids_ss.at[j], ids_rs.at[j], (d, row_at(j)))

    @pl.loop(1, row_count)
    def _(j):
        ids_copy(j).start()

    for copy in loads:
        copy.wait()

    def live(role, t):
        return t < count_ref[0, steps[role]]

    @pl.loop(0, tiles.shape[0])
    def _(k):
        for t in range(tps):
            tiles_t[k, t] = tiles[k, t].astype(f32).T.astype(bf16)

    weight_t[...] = weight[...].astype(f32).T.astype(bf16)

    def products(matrices, blocks, index_ref, role):
        for t in range(tps):
            index = jnp.where(live(role, t), index_ref[0, t, steps[role]], 0)
            prod[t] = dot(matrices[steps[role], t], blocks[index])

    def mixed(index_ref, role, wanted):
        value = None
        for t in range(tps):
            hit = live(role, t) & (index_ref[0, t, steps[role]] == wanted)
            term = prod[t] * jnp.where(hit, 1.0, 0.0).astype(f32)
            value = term if value is None else value + term
        return value

    def add_role(h, role, first):
        products(tiles, feats[h][role], source_ref, role)

        @pl.loop(0, row_count * cap)
        def _(slot):
            value = mixed(slot_ref, role, slot)
            acc[slot] = value if first else acc[slot] + value

    def part_copy(h, j):
        return remote(
            part_send.at[h, row_at(j)], part_recv.at[h, j], part_ss.at[h, j], part_rs.at[h, j], (d, row_at(j))
        )

    for h in range(halves):
        add_role(h, OWN, True)
        feat_copy(h, NEAR).wait_recv()
        feat_copy(h, PASSED).start()
        feat_copy(h, MATE).wait_recv()
        add_role(h, MATE, False)
        add_role(h, NEAR, False)
        feat_copy(h, FAR).wait_recv()
        add_role(h, FAR, False)
        feat_copy(h, PASSED).wait_recv()
        products(tiles, feats[h][PASSED], source_ref, PASSED)

        def finish(q):
            for c in range(cap):
                value = acc[q * cap + c] + mixed(slot_ref, PASSED, q * cap + c)
                part_send[h, q, c * B:(c + 1) * B, :] = value.astype(bf16)

        @pl.loop(1, row_count)
        def _(j):
            finish(row_at(j))
            part_copy(h, j).start()

        finish(r)
        part_recv[h, 0] = part_send[h, r]

    @pl.loop(1, row_count)
    def _(j):
        ids_copy(j).wait()

    def is_block(j, c, b):
        return ids_recv[j, c][0:1, :] == b

    for h in range(halves):
        @pl.loop(1, row_count)
        def _(j):
            part_copy(h, j).wait_recv()

        @pl.loop(0, nblk)
        def _(b):
            def gather(j, value):
                for c in range(cap):
                    term = part_recv[h, j, c * B:(c + 1) * B, :].astype(f32)
                    value = value + jnp.where(is_block(j, c, b), term, 0.0)
                return value

            value = lax.fori_loop(0, row_count, gather, jnp.zeros((B, LANES), f32), unroll=row_count <= 4)
            rows = pl.ds(pl.multiple_of(b * B, B), B)
            agg[h, rows, :] = value.astype(bf16)
            product = dot(value.astype(bf16), weight[h * LANES:(h + 1) * LANES, :])
            if h > 0:
                product = pre[rows, :] + product
            pre[rows, :] = product
            if h == halves - 1:
                sig = jax.nn.sigmoid(product)
                slope = sig * (1.0 + product * (1.0 - sig))
                pre_grad[rows, :] = (cot[rows, :].astype(f32) * slope).astype(bf16)
                act[rows, :] = (product * sig).astype(bf16)

    act_copy = pltpu.make_async_copy(act, act_out, out_sem.at[0])
    act_copy.start()

    def reply_copy(h, j):
        rows = pl.ds(pl.multiple_of(r * cap, cap), cap)
        return remote(
            reply_send.at[h, j], backs[h].at[rows], reply_ss.at[h, j], reply_rs.at[h, j], (d, row_at(-j))
        )

    chunk = wg_rows.shape[1]

    def w1_copy(j):
        return remote(wg_send.at[row_at(j)], wg_rows.at[j], w1_ss.at[j], w1_rs.at[j], (d, row_at(j)))

    def wg_first():
        for h in range(halves):
            wg_local[h * LANES:(h + 1) * LANES, :] = lax.dot_general(
                agg[h], pre_grad[...], (((0,), (0,)), ((), ())), preferred_element_type=f32
            )

        @pl.loop(0, row_count)
        def _(q):
            wg_send[q] = wg_local[pl.ds(pl.multiple_of(q * chunk, chunk), chunk), :].astype(bf16)

        @pl.loop(1, row_count)
        def _(j):
            w1_copy(j).start()

    for h in range(halves):
        product = dot(pre_grad[...], weight_t[:, h * LANES:(h + 1) * LANES])
        agg_grad[...] = product.astype(bf16)

        def reply(j):
            for c in range(cap):
                chosen = jnp.zeros((B, LANES), f32)
                for b in range(nblk):
                    chosen = jnp.where(is_block(j, c, b), agg_grad[b * B:(b + 1) * B, :].astype(f32), chosen)
                reply_send[h, j, c] = chosen.astype(bf16)

        @pl.loop(1, row_count)
        def _(j):
            reply(j)
            reply_copy(h, j).start()

        reply(0)
        backs[h][pl.ds(pl.multiple_of(r * cap, cap), cap)] = reply_send[h, 0]
        if h == 0:
            wg_first()


    pieces, high, wide = wg_pieces.shape
    scatter = pieces > 1

    def corner(i):
        return slice(i // (wg_local.shape[1] // wide) * high, (i // (wg_local.shape[1] // wide) + 1) * high), slice(
            i % (wg_local.shape[1] // wide) * wide, (i % (wg_local.shape[1] // wide) + 1) * wide
        )

    def w2_copy(j):
        src = wg_pieces.at[dom_at(j) if scatter else 0]
        return remote(src, wg_dom.at[j], w2_ss.at[j], w2_rs.at[j], (dom_at(j), r))

    def w3_copy(j):
        return remote(wg_mine.at[d], wg_mine.at[d], w3_ss.at[j], w3_rs.at[j], (dom_at(j), r))

    def w4_copy(i, j):
        at = dom_at(-i) if scatter else 0
        return remote(wg_mine.at[at], wg_all.at[r, at], w4_ss.at[i, j], w4_rs.at[i, j], (d, row_at(j)))

    def w4_start(i):
        @pl.loop(1, row_count)
        def _(j):
            w4_copy(i, j).start()

    wg_copy = pltpu.make_async_copy(wg_local, wg_out, out_sem.at[1 + halves])

    def wg_second():
        wg_chunk[...] = wg_local[pl.ds(pl.multiple_of(r * chunk, chunk), chunk), :]

        @pl.loop(1, row_count)
        def _(j):
            w1_copy(j).wait_recv()
            wg_chunk[...] += wg_rows[j].astype(f32)

        for i in range(pieces):
            wg_pieces[i] = wg_chunk[corner(i)].astype(bf16)

        @pl.loop(1, dom_count)
        def _(j):
            w2_copy(j).start()

    def g_copy(h, role):
        device = {NEAR: up_dev, FAR: down_dev, MATE: mate_dev, PASSED: mate_dev}[role]
        return remote(g_send.at[h, role], g_recv.at[h, role], g_ss.at[h, role], g_rs.at[h, role], device)

    for h in range(halves):
        @pl.loop(1, row_count)
        def _(j):
            reply_copy(h, j).wait_recv()

        def source_terms(role, target, extra=None):
            products(tiles_t, backs[h], slot_ref, role)

            @pl.loop(0, nblk)
            def _(b):
                rows = pl.ds(pl.multiple_of(b * B, B), B)
                value = mixed(source_ref, role, b)
                if extra is not None:
                    value = value + extra[rows, :].astype(f32)
                target[rows, :] = value.astype(target.dtype)

        for role in (PASSED, FAR):
            source_terms(role, g_send.at[h, role])
            g_copy(h, role).start()
        g_copy(h, PASSED).wait_recv()
        source_terms(NEAR, g_send.at[h, NEAR], g_recv.at[h, PASSED])
        g_copy(h, NEAR).start()
        source_terms(MATE, g_send.at[h, MATE])
        g_copy(h, MATE).start()
        source_terms(OWN, g_own.at[h])
        if h == 0:
            wg_second()

    if scatter:
        total_own = wg_pieces[d].astype(f32)
        for j in range(1, dom_count):
            w2_copy(j).wait_recv()
            total_own = total_own + wg_dom[j].astype(f32)
        wg_mine[d] = total_own.astype(bf16)

        @pl.loop(1, dom_count)
        def _(j):
            w3_copy(j).start()

        w4_start(0)

        @pl.loop(1, dom_count)
        def _(j):
            w3_copy(j).wait_recv()
            w4_start(j)

        @pl.loop(1, dom_count)
        def _(j):
            w3_copy(j).wait_send()
    else:
        wg_dom[0] = wg_pieces[0]

        @pl.loop(1, dom_count)
        def _(j):
            w2_copy(j).wait_recv()

        wg_mine[0] = lax.fori_loop(
            0, dom_count, lambda i, value: value + wg_dom[dom_at(-i)].astype(f32), jnp.zeros(wg_chunk.shape, f32)
        ).astype(bf16)
        w4_start(0)

    def grad_copy(h):
        return pltpu.make_async_copy(grad.at[h], grad_out.at[:, pl.ds(h * LANES, LANES)], out_sem.at[1 + h])

    for h in range(halves):
        for role in (MATE, NEAR, FAR):
            g_copy(h, role).wait_recv()
        value = g_own[h]
        for role in (MATE, NEAR, FAR):
            value = value + g_recv[h, role].astype(f32)
        grad[h] = value.astype(bf16)
        grad_copy(h).start()

    @pl.loop(0, dom_count if scatter else 1)
    def _(i):
        @pl.loop(1, row_count)
        def _(j):
            w4_copy(i, j).wait()

    wg_all[r] = wg_mine[...]

    @pl.loop(0, row_count)
    def _(q):
        for i in range(pieces):
            rows, cols = corner(i)
            here = pl.ds(pl.multiple_of(q * chunk + rows.start, high), high)
            wg_local[here, cols] = wg_all[q, i].astype(f32)

    wg_copy.start()

    act_copy.wait()
    wg_copy.wait()
    for h in range(halves):
        for role in (NEAR, FAR, MATE, PASSED):
            feat_copy(h, role).wait_send()
            g_copy(h, role).wait_send()
        grad_copy(h).wait()

        @pl.loop(1, row_count)
        def _(j):
            part_copy(h, j).wait_send()
            reply_copy(h, j).wait_send()

    @pl.loop(1, row_count)
    def _(j):
        w1_copy(j).wait_send()

    @pl.loop(1, dom_count)
    def _(j):
        w2_copy(j).wait_send()


def hand_over(a, b, c, to_a, to_b, to_c, in_a, in_b, in_c, sem):
    triples = ((a, in_a, to_a), (b, in_b, to_b), (c, in_c, to_c))
    reads = [pltpu.make_async_copy(x, y, sem.at[0, i]) for i, (x, y, _) in enumerate(triples)]
    writes = [pltpu.make_async_copy(y, z, sem.at[1, i]) for i, (_, y, z) in enumerate(triples)]
    for copy in reads:
        copy.start()
    for read, write in zip(reads, writes):
        read.wait()
        write.start()
    for copy in writes:
        copy.wait()


def per_device(
    features, weight, tile_values, tile_source, tile_slot, slot_block, tile_count, cotangent, *, dom_count, row_count
):
    nodes, channels = features.shape
    nblk = nodes // B
    halves = channels // LANES
    tps = tile_values.shape[2]
    slots = slot_block.shape[1]
    cap = slots // row_count
    chunk = channels // row_count
    scatter = chunk % 16 == 0 and chunk // 16 * halves == dom_count
    pieces, piece = (dom_count, (16, LANES)) if scatter else (1, (chunk, channels))
    smem = pl.BlockSpec(memory_space=pltpu.SMEM)
    anywhere = pl.BlockSpec(memory_space=pl.ANY)
    V = pltpu.VMEM
    dma = pltpu.SemaphoreType.DMA
    scratch = [
        V(tile_values.shape[1:], bf16), V(tile_values.shape[1:], bf16), V(weight.shape, bf16), V(weight.shape[::-1], bf16), V(cotangent.shape, bf16),
        V((tps, B, LANES), f32), V((slots, B, LANES), f32),
        *[V((nblk, B, LANES), bf16) for _ in range(10)],
        V((row_count, cap, 8, LANES), jnp.int32), V((row_count, cap, 8, LANES), jnp.int32),
        V((halves, row_count, cap * B, LANES), bf16), V((halves, row_count, cap * B, LANES), bf16),
        V((halves, nodes, LANES), bf16), V((nodes, channels), f32), V((nodes, channels), bf16), V((nodes, LANES), bf16),
        V((halves, row_count, cap, B, LANES), bf16), V((slots, B, LANES), bf16), V((slots, B, LANES), bf16),
        V((halves, nodes, LANES), f32), V((halves, 5, nodes, LANES), bf16), V((halves, 5, nodes, LANES), bf16),
        V((channels, channels), f32), V((row_count, chunk, channels), bf16), V((row_count, chunk, channels), bf16),
        V((chunk, channels), f32), V((pieces, *piece), bf16), V((dom_count, *piece), bf16), V((pieces, *piece), bf16),
        V((row_count, pieces, *piece), bf16),
        V((nodes, channels), bf16), V((halves, nodes, LANES), bf16),
        dma((3 + halves,)), dma((halves, 5)), dma((halves, 5)), dma((row_count,)), dma((row_count,)),
        dma((halves, row_count)), dma((halves, row_count)), dma((halves, row_count)), dma((halves, row_count)),
        dma((halves, 5)), dma((halves, 5)),
        dma((row_count,)), dma((row_count,)), dma((dom_count,)), dma((dom_count,)),
        dma((dom_count,)), dma((dom_count,)), dma((dom_count, row_count)), dma((dom_count, row_count)), dma((2 + halves,)),
    ]
    results = pl.pallas_call(
        functools.partial(kernel, dom_count, row_count),
        out_shape=(
            jax.ShapeDtypeStruct((nodes, channels), bf16),
            jax.ShapeDtypeStruct((nodes, channels), bf16),
            jax.ShapeDtypeStruct((channels, channels), f32),
        ),
        in_specs=[anywhere, anywhere, anywhere, smem, smem, smem, smem, anywhere],
        out_specs=(anywhere, anywhere, anywhere),
        scratch_shapes=scratch,
        compiler_params=pltpu.CompilerParams(
            collective_id=0, has_side_effects=True, vmem_limit_bytes=56 * 1024 * 1024
        ),
        name="graph_layer",
    )(
        features.reshape(nblk, B, channels), weight, tile_values,
        jnp.swapaxes(tile_source, 1, 2), jnp.swapaxes(tile_slot, 1, 2), slot_block, tile_count, cotangent,
    )
    return pl.pallas_call(
        hand_over,
        out_shape=tuple(jax.ShapeDtypeStruct(x.shape, x.dtype) for x in results),
        in_specs=[anywhere] * 3,
        out_specs=(anywhere,) * 3,
        scratch_shapes=[*[V(x.shape, x.dtype) for x in results], dma((2, 3))],
        compiler_params=pltpu.CompilerParams(vmem_limit_bytes=60 * 1024 * 1024),
        name="hand_over",
    )(*results)


def solution(mesh):
    both = P(("dom", "rows"))
    return jax.shard_map(
        functools.partial(per_device, dom_count=mesh.shape["dom"], row_count=mesh.shape["rows"]),
        mesh=mesh,
        in_specs=(both, P(), both, both, both, both, both, both),
        out_specs=(both, both, P()),
        check_vma=False,
    )
```

```python
import functools

import jax
import jax.numpy as jnp
from jax import lax
from jax.experimental import pallas as pl
from jax.experimental.pallas import tpu as pltpu
from jax.sharding import PartitionSpec as P

MESH = pl.DeviceIdType.MESH
B = 128
LANES = 128
OWN, NEAR, FAR, MATE, PASSED = range(5)
f32 = jnp.float32
bf16 = jnp.bfloat16


def dot(a, b):
    return jnp.dot(a, b, preferred_element_type=f32)


def kernel(
    dom_count, row_count,
    feat_ref, weight_ref, tiles_ref, source_ref, slot_ref, block_ref, count_ref, cot_ref,
    act_out, own_out, grad_out, wg_out,
    tiles, tiles_t, weight, weight_t, cot, prod, acc,
    own0, near0, far0, mate0, passed0, own1, near1, far1, mate1, passed1,
    ids_send, ids_recv,
    part_send, part_recv, agg, pre, pre_grad, agg_grad,
    reply_send, back0, back1,
    g_own, g_send, g_recv,
    wg_local, wg_send, wg_rows, wg_chunk, wg_pieces, wg_dom, wg_mine, act,
    load_sem, feat_ss, feat_rs, ids_ss, ids_rs, part_ss, part_rs, reply_ss, reply_rs,
    g_ss, g_rs, w1_ss, w1_rs, w2_ss, w2_rs, w3_ss, w3_rs, w4_ss, w4_rs, out_sem,
):
    d = lax.axis_index("dom")
    r = lax.axis_index("rows")
    parity = d % 2
    sigma = 1 - 2 * parity
    halves = feat_ref.shape[2] // LANES
    nblk = feat_ref.shape[0]
    tps = tiles_ref.shape[2]
    cap = block_ref.shape[1] // row_count
    nodes = nblk * B
    mate_dev = (d + sigma, r)
    up_dev = (lax.rem(d + 2 * sigma + dom_count, dom_count), r)
    down_dev = (lax.rem(d - 2 * sigma + dom_count, dom_count), r)
    steps = (2, 2 + 2 * sigma, 2 - 2 * sigma, 2 + sigma, 2 - sigma)
    feats = ((own0, near0, far0, mate0, passed0), (own1, near1, far1, mate1, passed1))
    backs = (back0, back1)

    def row_at(shift):
        return lax.rem(r + shift + row_count, row_count)

    def dom_at(shift):
        return lax.rem(d + shift + dom_count, dom_count)

    def remote(src, dst, ss, rs, device):
        return pltpu.make_async_remote_copy(
            src_ref=src, dst_ref=dst, send_sem=ss, recv_sem=rs, device_id=device, device_id_type=MESH
        )

    barrier = pltpu.get_barrier_semaphore()

    @pl.loop(1, dom_count)
    def _(j):
        pl.semaphore_signal(barrier, inc=1, device_id=(dom_at(j), r), device_id_type=MESH)

    @pl.loop(1, row_count)
    def _(j):
        pl.semaphore_signal(barrier, inc=1, device_id=(d, row_at(j)), device_id_type=MESH)

    def columns(h):
        return feat_ref.at[:, :, pl.ds(h * LANES, LANES)]

    loads = [
        pltpu.make_async_copy(tiles_ref.at[0], tiles, load_sem.at[0]),
        pltpu.make_async_copy(weight_ref, weight, load_sem.at[1]),
        pltpu.make_async_copy(cot_ref, cot, load_sem.at[2]),
    ]
    for h in range(halves):
        loads.append(pltpu.make_async_copy(columns(h), feats[h][OWN], load_sem.at[3 + h]))
    for copy in loads:
        copy.start()
    pl.semaphore_wait(barrier, dom_count + row_count - 2)

    def feat_copy(h, role):
        own = columns(h)
        if role == PASSED:
            src, device = feats[h][NEAR], mate_dev
        elif role == MATE:
            src, device = own, mate_dev
        elif role == FAR:
            src, device = own, up_dev
        else:
            src, device = own, down_dev
        return remote(src, feats[h][role], feat_ss.at[h, role], feat_rs.at[h, role], device)

    for h in range(halves):
        for role in (NEAR, FAR, MATE):
            feat_copy(h, role).start()

    @pl.loop(0, row_count)
    def _(q):
        for c in range(cap):
            ids_send[q, c] = jnp.full((8, LANES), block_ref[0, q * cap + c], jnp.int32)

    ids_recv[0] = ids_send[r]

    def ids_copy(j):
        return remote(ids_send.at[row_at(j)], ids_recv.at[j], ids_ss.at[j], ids_rs.at[j], (d, row_at(j)))

    @pl.loop(1, row_count)
    def _(j):
        ids_copy(j).start()

    for copy in loads:
        copy.wait()

    def live(role, t):
        return t < count_ref[0, steps[role]]

    @pl.loop(0, tiles.shape[0])
    def _(k):
        for t in range(tps):
            tiles_t[k, t] = tiles[k, t].astype(f32).T.astype(bf16)

    weight_t[...] = weight[...].astype(f32).T.astype(bf16)

    def products(matrices, blocks, index_ref, role):
        for t in range(tps):
            index = jnp.where(live(role, t), index_ref[0, t, steps[role]], 0)
            prod[t] = dot(matrices[steps[role], t], blocks[index])

    def mixed(index_ref, role, wanted):
        value = None
        for t in range(tps):
            hit = live(role, t) & (index_ref[0, t, steps[role]] == wanted)
            term = prod[t] * jnp.where(hit, 1.0, 0.0).astype(f32)
            value = term if value is None else value + term
        return value

    def add_role(h, role, first):
        products(tiles, feats[h][role], source_ref, role)

        @pl.loop(0, row_count * cap)
        def _(slot):
            value = mixed(slot_ref, role, slot)
            acc[slot] = value if first else acc[slot] + value

    def part_copy(h, j):
        return remote(
            part_send.at[h, row_at(j)], part_recv.at[h, j], part_ss.at[h, j], part_rs.at[h, j], (d, row_at(j))
        )

    for h in range(halves):
        add_role(h, OWN, True)
        feat_copy(h, NEAR).wait_recv()
        feat_copy(h, PASSED).start()
        feat_copy(h, MATE).wait_recv()
        add_role(h, MATE, False)
        add_role(h, NEAR, False)
        feat_copy(h, FAR).wait_recv()
        add_role(h, FAR, False)
        feat_copy(h, PASSED).wait_recv()
        products(tiles, feats[h][PASSED], source_ref, PASSED)

        def finish(q):
            for c in range(cap):
                value = acc[q * cap + c] + mixed(slot_ref, PASSED, q * cap + c)
                part_send[h, q, c * B:(c + 1) * B, :] = value.astype(bf16)

        @pl.loop(1, row_count)
        def _(j):
            finish(row_at(j))
            part_copy(h, j).start()

        finish(r)
        part_recv[h, 0] = part_send[h, r]

    @pl.loop(1, row_count)
    def _(j):
        ids_copy(j).wait()

    def is_block(j, c, b):
        return ids_recv[j, c][0:1, :] == b

    for h in range(halves):
        @pl.loop(1, row_count)
        def _(j):
            part_copy(h, j).wait_recv()

        @pl.loop(0, nblk)
        def _(b):
            def gather(j, value):
                for c in range(cap):
                    term = part_recv[h, j, c * B:(c + 1) * B, :].astype(f32)
                    value = value + jnp.where(is_block(j, c, b), term, 0.0)
                return value

            value = lax.fori_loop(0, row_count, gather, jnp.zeros((B, LANES), f32), unroll=row_count <= 4)
            rows = pl.ds(pl.multiple_of(b * B, B), B)
            agg[h, rows, :] = value.astype(bf16)
            product = dot(value.astype(bf16), weight[h * LANES:(h + 1) * LANES, :])
            if h > 0:
                product = pre[rows, :] + product
            pre[rows, :] = product
            if h == halves - 1:
                sig = jax.nn.sigmoid(product)
                slope = sig * (1.0 + product * (1.0 - sig))
                pre_grad[rows, :] = (cot[rows, :].astype(f32) * slope).astype(bf16)
                act[rows, :] = (product * sig).astype(bf16)

    act_copy = pltpu.make_async_copy(act, act_out, out_sem.at[0])
    act_copy.start()

    def reply_copy(h, j):
        rows = pl.ds(pl.multiple_of(r * cap, cap), cap)
        return remote(
            reply_send.at[h, j], backs[h].at[rows], reply_ss.at[h, j], reply_rs.at[h, j], (d, row_at(-j))
        )

    chunk = wg_rows.shape[1]

    def w1_copy(j):
        return remote(wg_send.at[row_at(j)], wg_rows.at[j], w1_ss.at[j], w1_rs.at[j], (d, row_at(j)))

    def wg_first():
        for h in range(halves):
            wg_local[h * LANES:(h + 1) * LANES, :] = lax.dot_general(
                agg[h], pre_grad[...], (((0,), (0,)), ((), ())), preferred_element_type=f32
            )

        @pl.loop(0, row_count)
        def _(q):
            wg_send[q] = wg_local[pl.ds(pl.multiple_of(q * chunk, chunk), chunk), :].astype(bf16)

        @pl.loop(1, row_count)
        def _(j):
            w1_copy(j).start()

    for h in range(halves):
        product = dot(pre_grad[...], weight_t[:, h * LANES:(h + 1) * LANES])
        agg_grad[...] = product.astype(bf16)

        def reply(j):
            for c in range(cap):
                chosen = jnp.zeros((B, LANES), f32)
                for b in range(nblk):
                    chosen = jnp.where(is_block(j, c, b), agg_grad[b * B:(b + 1) * B, :].astype(f32), chosen)
                reply_send[h, j, c] = chosen.astype(bf16)

        @pl.loop(1, row_count)
        def _(j):
            reply(j)
            reply_copy(h, j).start()

        reply(0)
        backs[h][pl.ds(pl.multiple_of(r * cap, cap), cap)] = reply_send[h, 0]
        if h == 0:
            wg_first()


    pieces, high, wide = wg_pieces.shape
    scatter = pieces > 1

    def corner(i):
        return corner_of(i, wg_local.shape[1], high, wide)

    def w2_copy(j):
        src = wg_pieces.at[dom_at(j) if scatter else 0]
        return remote(src, wg_dom.at[j], w2_ss.at[j], w2_rs.at[j], (dom_at(j), r))

    def w3_copy(j):
        return remote(wg_mine.at[d], wg_mine.at[d], w3_ss.at[j], w3_rs.at[j], (dom_at(j), r))

    def w4_copy(i, j):
        at = dom_at(-i) if scatter else 0
        return remote(wg_mine.at[at], wg_out.at[r, at], w4_ss.at[i, j], w4_rs.at[i, j], (d, row_at(j)))

    def w4_start(i):
        @pl.loop(1, row_count)
        def _(j):
            w4_copy(i, j).start()

    wg_copy = pltpu.make_async_copy(wg_mine, wg_out.at[r], out_sem.at[1 + halves])

    def wg_second():
        wg_chunk[...] = wg_local[pl.ds(pl.multiple_of(r * chunk, chunk), chunk), :]

        @pl.loop(1, row_count)
        def _(j):
            w1_copy(j).wait_recv()
            wg_chunk[...] += wg_rows[j].astype(f32)

        for i in range(pieces):
            wg_pieces[i] = wg_chunk[corner(i)].astype(bf16)

        @pl.loop(1, dom_count)
        def _(j):
            w2_copy(j).start()

    def g_copy(h, role):
        device = {NEAR: up_dev, FAR: down_dev, MATE: mate_dev, PASSED: mate_dev}[role]
        target = g_recv.at[h] if role == PASSED else grad_out.at[h, role - 1]
        return remote(g_send.at[h, role], target, g_ss.at[h, role], g_rs.at[h, role], device)

    def own_copy(h):
        return pltpu.make_async_copy(g_own.at[h], own_out.at[h], out_sem.at[1 + h])

    for h in range(halves):
        @pl.loop(1, row_count)
        def _(j):
            reply_copy(h, j).wait_recv()

        def source_terms(role, target, extra=None):
            products(tiles_t, backs[h], slot_ref, role)

            @pl.loop(0, nblk)
            def _(b):
                rows = pl.ds(pl.multiple_of(b * B, B), B)
                value = mixed(source_ref, role, b)
                if extra is not None:
                    value = value + extra[rows, :].astype(f32)
                target[rows, :] = value.astype(target.dtype)

        for role in (PASSED, FAR):
            source_terms(role, g_send.at[h, role])
            g_copy(h, role).start()
        g_copy(h, PASSED).wait_recv()
        source_terms(NEAR, g_send.at[h, NEAR], g_recv.at[h])
        g_copy(h, NEAR).start()
        source_terms(MATE, g_send.at[h, MATE])
        g_copy(h, MATE).start()
        source_terms(OWN, g_own.at[h])
        own_copy(h).start()
        if h == 0:
            wg_second()

    if scatter:
        total_own = wg_pieces[d].astype(f32)
        for j in range(1, dom_count):
            w2_copy(j).wait_recv()
            total_own = total_own + wg_dom[j].astype(f32)
        wg_mine[d] = total_own.astype(bf16)

        @pl.loop(1, dom_count)
        def _(j):
            w3_copy(j).start()

        w4_start(0)

        @pl.loop(1, dom_count)
        def _(j):
            w3_copy(j).wait_recv()
            w4_start(j)

        @pl.loop(1, dom_count)
        def _(j):
            w3_copy(j).wait_send()
    else:
        wg_dom[0] = wg_pieces[0]

        @pl.loop(1, dom_count)
        def _(j):
            w2_copy(j).wait_recv()

        wg_mine[0] = lax.fori_loop(
            0, dom_count, lambda i, value: value + wg_dom[dom_at(-i)].astype(f32), jnp.zeros(wg_chunk.shape, f32)
        ).astype(bf16)
        w4_start(0)

    wg_copy.start()

    for h in range(halves):
        for role in (MATE, NEAR, FAR):
            g_copy(h, role).wait_recv()

    @pl.loop(0, dom_count if scatter else 1)
    def _(i):
        @pl.loop(1, row_count)
        def _(j):
            w4_copy(i, j).wait()


    act_copy.wait()
    wg_copy.wait()
    for h in range(halves):
        for role in (NEAR, FAR, MATE, PASSED):
            feat_copy(h, role).wait_send()
            g_copy(h, role).wait_send()
        own_copy(h).wait()

        @pl.loop(1, row_count)
        def _(j):
            part_copy(h, j).wait_send()
            reply_copy(h, j).wait_send()

    @pl.loop(1, row_count)
    def _(j):
        w1_copy(j).wait_send()

    @pl.loop(1, dom_count)
    def _(j):
        w2_copy(j).wait_send()


def corner_of(i, channels, high, wide):
    across = channels // wide
    row, column = i // across * high, i % across * wide
    return slice(row, row + high), slice(column, column + wide)


def hand_over(act, own, grad, wg, to_act, to_grad, to_wg, in_act, in_own, in_grad, in_wg, sums, full, sem, out_sem):
    halves = own.shape[0]
    row_count, pieces, high, wide = wg.shape
    channels = full.shape[0]
    reads = []
    for h in range(halves):
        reads.append(pltpu.make_async_copy(own.at[h], in_own.at[h], sem.at[2 * h]))
        reads.append(pltpu.make_async_copy(grad.at[h], in_grad.at[h], sem.at[2 * h + 1]))
    reads.append(pltpu.make_async_copy(act, in_act, sem.at[2 * halves]))
    reads.append(pltpu.make_async_copy(wg, in_wg, sem.at[2 * halves + 1]))
    for copy in reads:
        copy.start()
    writes = []
    for h in range(halves):
        reads[2 * h].wait()
        reads[2 * h + 1].wait()
        value = in_own[h]
        for i in (2, 0, 1):
            value = value + in_grad[h, i].astype(f32)
        sums[h] = value.astype(bf16)
        writes.append(pltpu.make_async_copy(sums.at[h], to_grad.at[:, pl.ds(h * LANES, LANES)], out_sem.at[h]))
        writes[-1].start()
    reads[-2].wait()
    writes.append(pltpu.make_async_copy(in_act, to_act, out_sem.at[halves]))
    writes[-1].start()
    reads[-1].wait()
    chunk = channels // row_count
    for q in range(row_count):
        for i in range(pieces):
            rows, cols = corner_of(i, channels, high, wide)
            full[q * chunk + rows.start:q * chunk + rows.stop, cols] = in_wg[q, i].astype(f32)
    writes.append(pltpu.make_async_copy(full, to_wg, out_sem.at[halves + 1]))
    writes[-1].start()
    for copy in writes:
        copy.wait()


def per_device(
    features, weight, tile_values, tile_source, tile_slot, slot_block, tile_count, cotangent, *, dom_count, row_count
):
    nodes, channels = features.shape
    nblk = nodes // B
    halves = channels // LANES
    tps = tile_values.shape[2]
    slots = slot_block.shape[1]
    cap = slots // row_count
    chunk = channels // row_count
    scatter = chunk % 16 == 0 and chunk // 16 * halves == dom_count
    pieces, piece = (dom_count, (16, LANES)) if scatter else (1, (chunk, channels))
    smem = pl.BlockSpec(memory_space=pltpu.SMEM)
    anywhere = pl.BlockSpec(memory_space=pl.ANY)
    V = pltpu.VMEM
    dma = pltpu.SemaphoreType.DMA
    scratch = [
        V(tile_values.shape[1:], bf16), V(tile_values.shape[1:], bf16), V(weight.shape, bf16), V(weight.shape[::-1], bf16), V(cotangent.shape, bf16),
        V((tps, B, LANES), f32), V((slots, B, LANES), f32),
        *[V((nblk, B, LANES), bf16) for _ in range(10)],
        V((row_count, cap, 8, LANES), jnp.int32), V((row_count, cap, 8, LANES), jnp.int32),
        V((halves, row_count, cap * B, LANES), bf16), V((halves, row_count, cap * B, LANES), bf16),
        V((halves, nodes, LANES), bf16), V((nodes, channels), f32), V((nodes, channels), bf16), V((nodes, LANES), bf16),
        V((halves, row_count, cap, B, LANES), bf16), V((slots, B, LANES), bf16), V((slots, B, LANES), bf16),
        V((halves, nodes, LANES), f32), V((halves, 5, nodes, LANES), bf16), V((halves, nodes, LANES), bf16),
        V((channels, channels), f32), V((row_count, chunk, channels), bf16), V((row_count, chunk, channels), bf16),
        V((chunk, channels), f32), V((pieces, *piece), bf16), V((dom_count, *piece), bf16), V((pieces, *piece), bf16),
        V((nodes, channels), bf16),
        dma((3 + halves,)), dma((halves, 5)), dma((halves, 5)), dma((row_count,)), dma((row_count,)),
        dma((halves, row_count)), dma((halves, row_count)), dma((halves, row_count)), dma((halves, row_count)),
        dma((halves, 5)), dma((halves, 5)),
        dma((row_count,)), dma((row_count,)), dma((dom_count,)), dma((dom_count,)),
        dma((dom_count,)), dma((dom_count,)), dma((dom_count, row_count)), dma((dom_count, row_count)), dma((2 + halves,)),
    ]
    results = pl.pallas_call(
        functools.partial(kernel, dom_count, row_count),
        out_shape=(
            jax.ShapeDtypeStruct((nodes, channels), bf16),
            jax.ShapeDtypeStruct((halves, nodes, LANES), f32),
            jax.ShapeDtypeStruct((halves, 3, nodes, LANES), bf16),
            jax.ShapeDtypeStruct((row_count, pieces, *piece), bf16),
        ),
        in_specs=[anywhere, anywhere, anywhere, smem, smem, smem, smem, anywhere],
        out_specs=(anywhere,) * 4,
        scratch_shapes=scratch,
        compiler_params=pltpu.CompilerParams(
            collective_id=0, has_side_effects=True, vmem_limit_bytes=56 * 1024 * 1024
        ),
        name="graph_layer",
    )(
        features.reshape(nblk, B, channels), weight, tile_values,
        jnp.swapaxes(tile_source, 1, 2), jnp.swapaxes(tile_slot, 1, 2), slot_block, tile_count, cotangent,
    )
    return pl.pallas_call(
        hand_over,
        out_shape=(
            jax.ShapeDtypeStruct((nodes, channels), bf16),
            jax.ShapeDtypeStruct((nodes, channels), bf16),
            jax.ShapeDtypeStruct((channels, channels), f32),
        ),
        in_specs=[anywhere] * 4,
        out_specs=(anywhere,) * 3,
        scratch_shapes=[
            *[V(x.shape, x.dtype) for x in results],
            V((halves, nodes, LANES), bf16), V((channels, channels), f32), dma((2 * halves + 2,)), dma((halves + 2,)),
        ],
        compiler_params=pltpu.CompilerParams(vmem_limit_bytes=60 * 1024 * 1024),
        name="hand_over",
    )(*results)


def solution(mesh):
    both = P(("dom", "rows"))
    return jax.shard_map(
        functools.partial(per_device, dom_count=mesh.shape["dom"], row_count=mesh.shape["rows"]),
        mesh=mesh,
        in_specs=(both, P(), both, both, both, both, both, both),
        out_specs=(both, both, P()),
        check_vma=False,
    )
```

```python
import functools

import jax
import jax.numpy as jnp
from jax import lax
from jax.experimental import pallas as pl
from jax.experimental.pallas import tpu as pltpu
from jax.sharding import PartitionSpec as P

MESH = pl.DeviceIdType.MESH
B = 128
LANES = 128
OWN, NEAR, FAR, MATE, PASSED = range(5)
f32 = jnp.float32
bf16 = jnp.bfloat16


def dot(a, b):
    return jnp.dot(a, b, preferred_element_type=f32)


def kernel(
    dom_count, row_count,
    feat_ref, weight_ref, tiles_ref, source_ref, slot_ref, block_ref, count_ref, cot_ref,
    act_out, own_out, grad_out, wg_out,
    tiles, tiles_t, weight, weight_t, cot, prod, acc,
    own0, near0, far0, mate0, passed0, own1, near1, far1, mate1, passed1,
    ids_send, ids_recv,
    part_send, part_recv, agg, pre, pre_grad, agg_grad,
    reply_send, back0, back1,
    g_own, g_send, g_recv,
    wg_local, wg_send, wg_rows, wg_chunk, wg_pieces, wg_dom, wg_mine, act,
    load_sem, feat_ss, feat_rs, ids_ss, ids_rs, part_ss, part_rs, reply_ss, reply_rs,
    g_ss, g_rs, w1_ss, w1_rs, w2_ss, w2_rs, w3_ss, w3_rs, w4_ss, w4_rs, out_sem,
):
    d = lax.axis_index("dom")
    r = lax.axis_index("rows")
    parity = d % 2
    sigma = 1 - 2 * parity
    halves = feat_ref.shape[2] // LANES
    nblk = feat_ref.shape[0]
    tps = tiles_ref.shape[2]
    cap = block_ref.shape[1] // row_count
    nodes = nblk * B
    mate_dev = (d + sigma, r)
    up_dev = (lax.rem(d + 2 * sigma + dom_count, dom_count), r)
    down_dev = (lax.rem(d - 2 * sigma + dom_count, dom_count), r)
    steps = (2, 2 + 2 * sigma, 2 - 2 * sigma, 2 + sigma, 2 - sigma)
    feats = ((own0, near0, far0, mate0, passed0), (own1, near1, far1, mate1, passed1))
    backs = (back0, back1)

    def row_at(shift):
        return lax.rem(r + shift + row_count, row_count)

    def dom_at(shift):
        return lax.rem(d + shift + dom_count, dom_count)

    def remote(src, dst, ss, rs, device):
        return pltpu.make_async_remote_copy(
            src_ref=src, dst_ref=dst, send_sem=ss, recv_sem=rs, device_id=device, device_id_type=MESH
        )

    barrier = pltpu.get_barrier_semaphore()

    @pl.loop(1, dom_count)
    def _(j):
        pl.semaphore_signal(barrier, inc=1, device_id=(dom_at(j), r), device_id_type=MESH)

    @pl.loop(1, row_count)
    def _(j):
        pl.semaphore_signal(barrier, inc=1, device_id=(d, row_at(j)), device_id_type=MESH)

    def columns(h):
        return feat_ref.at[:, :, pl.ds(h * LANES, LANES)]

    loads = [
        pltpu.make_async_copy(tiles_ref.at[0], tiles, load_sem.at[0]),
        pltpu.make_async_copy(weight_ref, weight, load_sem.at[1]),
        pltpu.make_async_copy(cot_ref, cot, load_sem.at[2]),
    ]
    for h in range(halves):
        loads.append(pltpu.make_async_copy(columns(h), feats[h][OWN], load_sem.at[3 + h]))
    for copy in loads:
        copy.start()
    pl.semaphore_wait(barrier, dom_count + row_count - 2)

    def feat_copy(h, role, b=None):
        own = columns(h)
        if role == PASSED:
            src, device = feats[h][NEAR], mate_dev
        elif role == MATE:
            src, device = own, mate_dev
        elif role == FAR:
            src, device = own, up_dev
        else:
            src, device = own, down_dev
        if b is None:
            return remote(src, feats[h][role], feat_ss.at[h, role, 0], feat_rs.at[h, role, 0], device)
        if role == NEAR:
            src = feat_ref.at[b, :, pl.ds(h * LANES, LANES)]
        else:
            src = src.at[b]
        return remote(src, feats[h][role].at[b], feat_ss.at[h, role, b], feat_rs.at[h, role, b], device)

    for h in range(halves):
        @pl.loop(0, nblk)
        def _(b):
            feat_copy(h, NEAR, b).start()

        for role in (FAR, MATE):
            feat_copy(h, role).start()

    @pl.loop(0, row_count)
    def _(q):
        for c in range(cap):
            ids_send[q, c] = jnp.full((8, LANES), block_ref[0, q * cap + c], jnp.int32)

    ids_recv[0] = ids_send[r]

    def ids_copy(j):
        return remote(ids_send.at[row_at(j)], ids_recv.at[j], ids_ss.at[j], ids_rs.at[j], (d, row_at(j)))

    @pl.loop(1, row_count)
    def _(j):
        ids_copy(j).start()

    for copy in loads:
        copy.wait()

    def live(role, t):
        return t < count_ref[0, steps[role]]

    @pl.loop(0, tiles.shape[0])
    def _(k):
        for t in range(tps):
            tiles_t[k, t] = tiles[k, t].astype(f32).T.astype(bf16)

    weight_t[...] = weight[...].astype(f32).T.astype(bf16)

    def products(matrices, blocks, index_ref, role):
        for t in range(tps):
            index = jnp.where(live(role, t), index_ref[0, t, steps[role]], 0)
            prod[t] = dot(matrices[steps[role], t], blocks[index])

    def mixed(index_ref, role, wanted):
        value = None
        for t in range(tps):
            hit = live(role, t) & (index_ref[0, t, steps[role]] == wanted)
            term = prod[t] * jnp.where(hit, 1.0, 0.0).astype(f32)
            value = term if value is None else value + term
        return value

    def add_role(h, role, first):
        products(tiles, feats[h][role], source_ref, role)

        @pl.loop(0, row_count * cap)
        def _(slot):
            value = mixed(slot_ref, role, slot)
            acc[slot] = value if first else acc[slot] + value

    def part_copy(h, j):
        return remote(
            part_send.at[h, row_at(j)], part_recv.at[h, j], part_ss.at[h, j], part_rs.at[h, j], (d, row_at(j))
        )

    for h in range(halves):
        add_role(h, OWN, True)

        @pl.loop(0, nblk)
        def _(b):
            feat_copy(h, NEAR, b).wait_recv()
            feat_copy(h, PASSED, b).start()

        feat_copy(h, MATE).wait_recv()
        add_role(h, MATE, False)
        add_role(h, NEAR, False)
        feat_copy(h, FAR).wait_recv()
        add_role(h, FAR, False)

        @pl.loop(0, nblk)
        def _(b):
            feat_copy(h, PASSED, b).wait_recv()

        products(tiles, feats[h][PASSED], source_ref, PASSED)

        def finish(q):
            for c in range(cap):
                value = acc[q * cap + c] + mixed(slot_ref, PASSED, q * cap + c)
                part_send[h, q, c * B:(c + 1) * B, :] = value.astype(bf16)

        @pl.loop(1, row_count)
        def _(j):
            finish(row_at(j))
            part_copy(h, j).start()

        finish(r)
        part_recv[h, 0] = part_send[h, r]

    @pl.loop(1, row_count)
    def _(j):
        ids_copy(j).wait()

    def is_block(j, c, b):
        return ids_recv[j, c][0:1, :] == b

    for h in range(halves):
        @pl.loop(1, row_count)
        def _(j):
            part_copy(h, j).wait_recv()

        @pl.loop(0, nblk)
        def _(b):
            def gather(j, value):
                for c in range(cap):
                    term = part_recv[h, j, c * B:(c + 1) * B, :].astype(f32)
                    value = value + jnp.where(is_block(j, c, b), term, 0.0)
                return value

            value = lax.fori_loop(0, row_count, gather, jnp.zeros((B, LANES), f32), unroll=row_count <= 4)
            rows = pl.ds(pl.multiple_of(b * B, B), B)
            agg[h, rows, :] = value.astype(bf16)
            product = dot(value.astype(bf16), weight[h * LANES:(h + 1) * LANES, :])
            if h > 0:
                product = pre[rows, :] + product
            pre[rows, :] = product
            if h == halves - 1:
                sig = jax.nn.sigmoid(product)
                slope = sig * (1.0 + product * (1.0 - sig))
                pre_grad[rows, :] = (cot[rows, :].astype(f32) * slope).astype(bf16)
                act[rows, :] = (product * sig).astype(bf16)

    act_copy = pltpu.make_async_copy(act, act_out, out_sem.at[0])
    act_copy.start()

    def reply_copy(h, j):
        rows = pl.ds(pl.multiple_of(r * cap, cap), cap)
        return remote(
            reply_send.at[h, j], backs[h].at[rows], reply_ss.at[h, j], reply_rs.at[h, j], (d, row_at(-j))
        )

    chunk = wg_rows.shape[1]

    def w1_copy(j):
        return remote(wg_send.at[row_at(j)], wg_rows.at[j], w1_ss.at[j], w1_rs.at[j], (d, row_at(j)))

    def wg_first():
        for h in range(halves):
            wg_local[h * LANES:(h + 1) * LANES, :] = lax.dot_general(
                agg[h], pre_grad[...], (((0,), (0,)), ((), ())), preferred_element_type=f32
            )

        @pl.loop(0, row_count)
        def _(q):
            wg_send[q] = wg_local[pl.ds(pl.multiple_of(q * chunk, chunk), chunk), :].astype(bf16)

        @pl.loop(1, row_count)
        def _(j):
            w1_copy(j).start()

    for h in range(halves):
        product = dot(pre_grad[...], weight_t[:, h * LANES:(h + 1) * LANES])
        agg_grad[...] = product.astype(bf16)

        def reply(j):
            for c in range(cap):
                chosen = jnp.zeros((B, LANES), f32)
                for b in range(nblk):
                    chosen = jnp.where(is_block(j, c, b), agg_grad[b * B:(b + 1) * B, :].astype(f32), chosen)
                reply_send[h, j, c] = chosen.astype(bf16)

        @pl.loop(1, row_count)
        def _(j):
            reply(j)
            reply_copy(h, j).start()

        reply(0)
        backs[h][pl.ds(pl.multiple_of(r * cap, cap), cap)] = reply_send[h, 0]
        if h == 0:
            wg_first()


    pieces, high, wide = wg_pieces.shape
    scatter = pieces > 1

    def corner(i):
        return corner_of(i, wg_local.shape[1], high, wide)

    def w2_copy(j):
        src = wg_pieces.at[dom_at(j) if scatter else 0]
        return remote(src, wg_dom.at[j], w2_ss.at[j], w2_rs.at[j], (dom_at(j), r))

    def w3_copy(j):
        return remote(wg_mine.at[d], wg_mine.at[d], w3_ss.at[j], w3_rs.at[j], (dom_at(j), r))

    def w4_copy(i, j):
        at = dom_at(-i) if scatter else 0
        return remote(wg_mine.at[at], wg_out.at[r, at], w4_ss.at[i, j], w4_rs.at[i, j], (d, row_at(j)))

    def w4_start(i):
        @pl.loop(1, row_count)
        def _(j):
            w4_copy(i, j).start()

    wg_copy = pltpu.make_async_copy(wg_mine, wg_out.at[r], out_sem.at[1 + halves])

    def wg_second():
        wg_chunk[...] = wg_local[pl.ds(pl.multiple_of(r * chunk, chunk), chunk), :]

        @pl.loop(1, row_count)
        def _(j):
            w1_copy(j).wait_recv()
            wg_chunk[...] += wg_rows[j].astype(f32)

        for i in range(pieces):
            wg_pieces[i] = wg_chunk[corner(i)].astype(bf16)

        @pl.loop(1, dom_count)
        def _(j):
            w2_copy(j).start()

    def g_copy(h, role, b=None):
        device = {NEAR: up_dev, FAR: down_dev, MATE: mate_dev, PASSED: mate_dev}[role]
        target = g_recv.at[h] if role == PASSED else grad_out.at[h, role - 1]
        if b is None:
            return remote(g_send.at[h, role], target, g_ss.at[h, role, 0], g_rs.at[h, role, 0], device)
        rows = pl.ds(pl.multiple_of(b * B, B), B)
        return remote(g_send.at[h, role, rows], target.at[rows], g_ss.at[h, role, b], g_rs.at[h, role, b], device)

    def own_copy(h):
        return pltpu.make_async_copy(g_own.at[h], own_out.at[h], out_sem.at[1 + h])

    for h in range(halves):
        @pl.loop(1, row_count)
        def _(j):
            reply_copy(h, j).wait_recv()

        def source_terms(role, target):
            products(tiles_t, backs[h], slot_ref, role)

            @pl.loop(0, nblk)
            def _(b):
                rows = pl.ds(pl.multiple_of(b * B, B), B)
                value = mixed(source_ref, role, b)
                if role == NEAR:
                    g_copy(h, PASSED, b).wait_recv()
                    value = value + g_recv[h, rows, :].astype(f32)
                target[rows, :] = value.astype(target.dtype)
                if role in (PASSED, NEAR):
                    g_copy(h, role, b).start()

        source_terms(PASSED, g_send.at[h, PASSED])
        source_terms(FAR, g_send.at[h, FAR])
        g_copy(h, FAR).start()
        source_terms(NEAR, g_send.at[h, NEAR])
        source_terms(MATE, g_send.at[h, MATE])
        g_copy(h, MATE).start()
        source_terms(OWN, g_own.at[h])
        own_copy(h).start()
        if h == 0:
            wg_second()

    if scatter:
        total_own = wg_pieces[d].astype(f32)
        for j in range(1, dom_count):
            w2_copy(j).wait_recv()
            total_own = total_own + wg_dom[j].astype(f32)
        wg_mine[d] = total_own.astype(bf16)

        @pl.loop(1, dom_count)
        def _(j):
            w3_copy(j).start()

        w4_start(0)

        @pl.loop(1, dom_count)
        def _(j):
            w3_copy(j).wait_recv()
            w4_start(j)

        @pl.loop(1, dom_count)
        def _(j):
            w3_copy(j).wait_send()
    else:
        wg_dom[0] = wg_pieces[0]

        @pl.loop(1, dom_count)
        def _(j):
            w2_copy(j).wait_recv()

        wg_mine[0] = lax.fori_loop(
            0, dom_count, lambda i, value: value + wg_dom[dom_at(-i)].astype(f32), jnp.zeros(wg_chunk.shape, f32)
        ).astype(bf16)
        w4_start(0)

    wg_copy.start()

    for h in range(halves):
        for role in (MATE, FAR):
            g_copy(h, role).wait_recv()

        @pl.loop(0, nblk)
        def _(b):
            g_copy(h, NEAR, b).wait_recv()


    @pl.loop(0, dom_count if scatter else 1)
    def _(i):
        @pl.loop(1, row_count)
        def _(j):
            w4_copy(i, j).wait()


    act_copy.wait()
    wg_copy.wait()
    for h in range(halves):
        for role in (FAR, MATE):
            feat_copy(h, role).wait_send()
            g_copy(h, role).wait_send()

        @pl.loop(0, nblk)
        def _(b):
            for role in (NEAR, PASSED):
                feat_copy(h, role, b).wait_send()
                g_copy(h, role, b).wait_send()

        own_copy(h).wait()

        @pl.loop(1, row_count)
        def _(j):
            part_copy(h, j).wait_send()
            reply_copy(h, j).wait_send()

    @pl.loop(1, row_count)
    def _(j):
        w1_copy(j).wait_send()

    @pl.loop(1, dom_count)
    def _(j):
        w2_copy(j).wait_send()


def corner_of(i, channels, high, wide):
    across = channels // wide
    row, column = i // across * high, i % across * wide
    return slice(row, row + high), slice(column, column + wide)


def hand_over(act, own, grad, wg, to_act, to_grad, to_wg, in_act, in_own, in_grad, in_wg, sums, full, sem, out_sem):
    halves = own.shape[0]
    row_count, pieces, high, wide = wg.shape
    channels = full.shape[0]
    reads = []
    for h in range(halves):
        reads.append(pltpu.make_async_copy(own.at[h], in_own.at[h], sem.at[2 * h]))
        reads.append(pltpu.make_async_copy(grad.at[h], in_grad.at[h], sem.at[2 * h + 1]))
    reads.append(pltpu.make_async_copy(act, in_act, sem.at[2 * halves]))
    reads.append(pltpu.make_async_copy(wg, in_wg, sem.at[2 * halves + 1]))
    for copy in reads:
        copy.start()
    writes = []
    for h in range(halves):
        reads[2 * h].wait()
        reads[2 * h + 1].wait()
        value = in_own[h]
        for i in (2, 0, 1):
            value = value + in_grad[h, i].astype(f32)
        sums[h] = value.astype(bf16)
        writes.append(pltpu.make_async_copy(sums.at[h], to_grad.at[:, pl.ds(h * LANES, LANES)], out_sem.at[h]))
        writes[-1].start()
    reads[-2].wait()
    writes.append(pltpu.make_async_copy(in_act, to_act, out_sem.at[halves]))
    writes[-1].start()
    reads[-1].wait()
    chunk = channels // row_count
    for q in range(row_count):
        for i in range(pieces):
            rows, cols = corner_of(i, channels, high, wide)
            full[q * chunk + rows.start:q * chunk + rows.stop, cols] = in_wg[q, i].astype(f32)
    writes.append(pltpu.make_async_copy(full, to_wg, out_sem.at[halves + 1]))
    writes[-1].start()
    for copy in writes:
        copy.wait()


def per_device(
    features, weight, tile_values, tile_source, tile_slot, slot_block, tile_count, cotangent, *, dom_count, row_count
):
    nodes, channels = features.shape
    nblk = nodes // B
    halves = channels // LANES
    tps = tile_values.shape[2]
    slots = slot_block.shape[1]
    cap = slots // row_count
    chunk = channels // row_count
    scatter = chunk % 16 == 0 and chunk // 16 * halves == dom_count
    pieces, piece = (dom_count, (16, LANES)) if scatter else (1, (chunk, channels))
    smem = pl.BlockSpec(memory_space=pltpu.SMEM)
    anywhere = pl.BlockSpec(memory_space=pl.ANY)
    V = pltpu.VMEM
    dma = pltpu.SemaphoreType.DMA
    scratch = [
        V(tile_values.shape[1:], bf16), V(tile_values.shape[1:], bf16), V(weight.shape, bf16), V(weight.shape[::-1], bf16), V(cotangent.shape, bf16),
        V((tps, B, LANES), f32), V((slots, B, LANES), f32),
        *[V((nblk, B, LANES), bf16) for _ in range(10)],
        V((row_count, cap, 8, LANES), jnp.int32), V((row_count, cap, 8, LANES), jnp.int32),
        V((halves, row_count, cap * B, LANES), bf16), V((halves, row_count, cap * B, LANES), bf16),
        V((halves, nodes, LANES), bf16), V((nodes, channels), f32), V((nodes, channels), bf16), V((nodes, LANES), bf16),
        V((halves, row_count, cap, B, LANES), bf16), V((slots, B, LANES), bf16), V((slots, B, LANES), bf16),
        V((halves, nodes, LANES), f32), V((halves, 5, nodes, LANES), bf16), V((halves, nodes, LANES), bf16),
        V((channels, channels), f32), V((row_count, chunk, channels), bf16), V((row_count, chunk, channels), bf16),
        V((chunk, channels), f32), V((pieces, *piece), bf16), V((dom_count, *piece), bf16), V((pieces, *piece), bf16),
        V((nodes, channels), bf16),
        dma((3 + halves,)), dma((halves, 5, nblk)), dma((halves, 5, nblk)), dma((row_count,)), dma((row_count,)),
        dma((halves, row_count)), dma((halves, row_count)), dma((halves, row_count)), dma((halves, row_count)),
        dma((halves, 5, nblk)), dma((halves, 5, nblk)),
        dma((row_count,)), dma((row_count,)), dma((dom_count,)), dma((dom_count,)),
        dma((dom_count,)), dma((dom_count,)), dma((dom_count, row_count)), dma((dom_count, row_count)), dma((2 + halves,)),
    ]
    results = pl.pallas_call(
        functools.partial(kernel, dom_count, row_count),
        out_shape=(
            jax.ShapeDtypeStruct((nodes, channels), bf16),
            jax.ShapeDtypeStruct((halves, nodes, LANES), f32),
            jax.ShapeDtypeStruct((halves, 3, nodes, LANES), bf16),
            jax.ShapeDtypeStruct((row_count, pieces, *piece), bf16),
        ),
        in_specs=[anywhere, anywhere, anywhere, smem, smem, smem, smem, anywhere],
        out_specs=(anywhere,) * 4,
        scratch_shapes=scratch,
        compiler_params=pltpu.CompilerParams(
            collective_id=0, has_side_effects=True, vmem_limit_bytes=56 * 1024 * 1024
        ),
        name="graph_layer",
    )(
        features.reshape(nblk, B, channels), weight, tile_values,
        jnp.swapaxes(tile_source, 1, 2), jnp.swapaxes(tile_slot, 1, 2), slot_block, tile_count, cotangent,
    )
    return pl.pallas_call(
        hand_over,
        out_shape=(
            jax.ShapeDtypeStruct((nodes, channels), bf16),
            jax.ShapeDtypeStruct((nodes, channels), bf16),
            jax.ShapeDtypeStruct((channels, channels), f32),
        ),
        in_specs=[anywhere] * 4,
        out_specs=(anywhere,) * 3,
        scratch_shapes=[
            *[V(x.shape, x.dtype) for x in results],
            V((halves, nodes, LANES), bf16), V((channels, channels), f32), dma((2 * halves + 2,)), dma((halves + 2,)),
        ],
        compiler_params=pltpu.CompilerParams(vmem_limit_bytes=60 * 1024 * 1024),
        name="hand_over",
    )(*results)


def solution(mesh):
    both = P(("dom", "rows"))
    return jax.shard_map(
        functools.partial(per_device, dom_count=mesh.shape["dom"], row_count=mesh.shape["rows"]),
        mesh=mesh,
        in_specs=(both, P(), both, both, both, both, both, both),
        out_specs=(both, both, P()),
        check_vma=False,
    )
```

```python
import functools

import jax
import jax.numpy as jnp
from jax import lax
from jax.experimental import pallas as pl
from jax.experimental.pallas import tpu as pltpu
from jax.sharding import PartitionSpec as P

MESH = pl.DeviceIdType.MESH
B = 128
LANES = 128
OWN, NEAR, FAR, MATE, PASSED = range(5)
f32 = jnp.float32
bf16 = jnp.bfloat16


def dot(a, b):
    return jnp.dot(a, b, preferred_element_type=f32)


def kernel(
    dom_count, row_count,
    feat_ref, weight_ref, tiles_ref, source_ref, slot_ref, block_ref, count_ref, cot_ref,
    act_out, own_out, grad_out, wg_out,
    tiles, tiles_t, weight, weight_t, cot, prod, acc,
    own0, near0, far0, mate0, passed0, own1, near1, far1, mate1, passed1,
    ids_send, ids_recv,
    part_send, part_recv, agg, pre, pre_grad, agg_grad,
    reply_send, back0, back1,
    g_own, g_send, g_recv,
    wg_local, wg_send, wg_rows, wg_chunk, wg_pieces, wg_dom, wg_mine, act,
    load_sem, feat_ss, feat_rs, ids_ss, ids_rs, part_ss, part_rs, reply_ss, reply_rs,
    g_ss, g_rs, w1_ss, w1_rs, w2_ss, w2_rs, w3_ss, w3_rs, w4_ss, w4_rs, out_sem,
):
    d = lax.axis_index("dom")
    r = lax.axis_index("rows")
    parity = d % 2
    sigma = 1 - 2 * parity
    halves = feat_ref.shape[2] // LANES
    nblk = feat_ref.shape[0]
    tps = tiles_ref.shape[2]
    cap = block_ref.shape[1] // row_count
    nodes = nblk * B
    mate_dev = (d + sigma, r)
    up_dev = (lax.rem(d + 2 * sigma + dom_count, dom_count), r)
    down_dev = (lax.rem(d - 2 * sigma + dom_count, dom_count), r)
    steps = (2, 2 + 2 * sigma, 2 - 2 * sigma, 2 + sigma, 2 - sigma)
    feats = ((own0, near0, far0, mate0, passed0), (own1, near1, far1, mate1, passed1))
    backs = (back0, back1)

    def row_at(shift):
        return lax.rem(r + shift + row_count, row_count)

    def dom_at(shift):
        return lax.rem(d + shift + dom_count, dom_count)

    def remote(src, dst, ss, rs, device):
        return pltpu.make_async_remote_copy(
            src_ref=src, dst_ref=dst, send_sem=ss, recv_sem=rs, device_id=device, device_id_type=MESH
        )

    barrier = pltpu.get_barrier_semaphore()

    @pl.loop(1, dom_count)
    def _(j):
        pl.semaphore_signal(barrier, inc=1, device_id=(dom_at(j), r), device_id_type=MESH)

    @pl.loop(1, row_count)
    def _(j):
        pl.semaphore_signal(barrier, inc=1, device_id=(d, row_at(j)), device_id_type=MESH)

    def columns(h):
        return feat_ref.at[:, :, pl.ds(h * LANES, LANES)]

    loads = [
        pltpu.make_async_copy(tiles_ref.at[0], tiles, load_sem.at[0]),
        pltpu.make_async_copy(weight_ref, weight, load_sem.at[1]),
        pltpu.make_async_copy(cot_ref, cot, load_sem.at[2]),
    ]
    for h in range(halves):
        loads.append(pltpu.make_async_copy(columns(h), feats[h][OWN], load_sem.at[3 + h]))
    for copy in loads[3:] + loads[:3]:
        copy.start()
    for copy in loads[3:]:
        copy.wait()
    pl.semaphore_wait(barrier, dom_count + row_count - 2)

    def feat_copy(h, role):
        own = feats[h][OWN]
        if role == PASSED:
            src, device = feats[h][NEAR], mate_dev
        elif role == MATE:
            src, device = own, mate_dev
        elif role == FAR:
            src, device = own, up_dev
        else:
            src, device = own, down_dev
        return remote(src, feats[h][role], feat_ss.at[h, role], feat_rs.at[h, role], device)

    for h in range(halves):
        for role in (NEAR, FAR, MATE):
            feat_copy(h, role).start()

    @pl.loop(0, row_count)
    def _(q):
        for c in range(cap):
            ids_send[q, c] = jnp.full((8, LANES), block_ref[0, q * cap + c], jnp.int32)

    ids_recv[0] = ids_send[r]

    def ids_copy(j):
        return remote(ids_send.at[row_at(j)], ids_recv.at[j], ids_ss.at[j], ids_rs.at[j], (d, row_at(j)))

    @pl.loop(1, row_count)
    def _(j):
        ids_copy(j).start()

    for copy in loads[:3]:
        copy.wait()

    def live(role, t):
        return t < count_ref[0, steps[role]]

    @pl.loop(0, tiles.shape[0])
    def _(k):
        for t in range(tps):
            tiles_t[k, t] = tiles[k, t].astype(f32).T.astype(bf16)

    weight_t[...] = weight[...].astype(f32).T.astype(bf16)

    def products(matrices, blocks, index_ref, role):
        for t in range(tps):
            index = jnp.where(live(role, t), index_ref[0, t, steps[role]], 0)
            prod[t] = dot(matrices[steps[role], t], blocks[index])

    def mixed(index_ref, role, wanted):
        value = None
        for t in range(tps):
            hit = live(role, t) & (index_ref[0, t, steps[role]] == wanted)
            term = prod[t] * jnp.where(hit, 1.0, 0.0).astype(f32)
            value = term if value is None else value + term
        return value

    def add_role(h, role, first):
        products(tiles, feats[h][role], source_ref, role)

        @pl.loop(0, row_count * cap)
        def _(slot):
            value = mixed(slot_ref, role, slot)
            acc[slot] = value if first else acc[slot] + value

    def part_copy(h, j):
        return remote(
            part_send.at[h, row_at(j)], part_recv.at[h, j], part_ss.at[h, j], part_rs.at[h, j], (d, row_at(j))
        )

    for h in range(halves):
        add_role(h, OWN, True)
        feat_copy(h, NEAR).wait_recv()
        feat_copy(h, PASSED).start()
        feat_copy(h, MATE).wait_recv()
        add_role(h, MATE, False)
        add_role(h, NEAR, False)
        feat_copy(h, FAR).wait_recv()
        add_role(h, FAR, False)
        feat_copy(h, PASSED).wait_recv()
        products(tiles, feats[h][PASSED], source_ref, PASSED)

        def finish(q):
            for c in range(cap):
                value = acc[q * cap + c] + mixed(slot_ref, PASSED, q * cap + c)
                part_send[h, q, c * B:(c + 1) * B, :] = value.astype(bf16)

        @pl.loop(1, row_count)
        def _(j):
            finish(row_at(j))
            part_copy(h, j).start()

        finish(r)
        part_recv[h, 0] = part_send[h, r]

    @pl.loop(1, row_count)
    def _(j):
        ids_copy(j).wait()

    def is_block(j, c, b):
        return ids_recv[j, c][0:1, :] == b

    for h in range(halves):
        @pl.loop(1, row_count)
        def _(j):
            part_copy(h, j).wait_recv()

        @pl.loop(0, nblk)
        def _(b):
            def gather(j, value):
                for c in range(cap):
                    term = part_recv[h, j, c * B:(c + 1) * B, :].astype(f32)
                    value = value + jnp.where(is_block(j, c, b), term, 0.0)
                return value

            value = lax.fori_loop(0, row_count, gather, jnp.zeros((B, LANES), f32), unroll=row_count <= 4)
            rows = pl.ds(pl.multiple_of(b * B, B), B)
            agg[h, rows, :] = value.astype(bf16)
            product = dot(value.astype(bf16), weight[h * LANES:(h + 1) * LANES, :])
            if h > 0:
                product = pre[rows, :] + product
            pre[rows, :] = product
            if h == halves - 1:
                sig = jax.nn.sigmoid(product)
                slope = sig * (1.0 + product * (1.0 - sig))
                pre_grad[rows, :] = (cot[rows, :].astype(f32) * slope).astype(bf16)
                act[rows, :] = (product * sig).astype(bf16)

    act_copy = pltpu.make_async_copy(act, act_out, out_sem.at[0])
    act_copy.start()

    def reply_copy(h, j):
        rows = pl.ds(pl.multiple_of(r * cap, cap), cap)
        return remote(
            reply_send.at[h, j], backs[h].at[rows], reply_ss.at[h, j], reply_rs.at[h, j], (d, row_at(-j))
        )

    chunk = wg_rows.shape[1]

    def w1_copy(j):
        return remote(wg_send.at[row_at(j)], wg_rows.at[j], w1_ss.at[j], w1_rs.at[j], (d, row_at(j)))

    def wg_first():
        for h in range(halves):
            wg_local[h * LANES:(h + 1) * LANES, :] = lax.dot_general(
                agg[h], pre_grad[...], (((0,), (0,)), ((), ())), preferred_element_type=f32
            )

        @pl.loop(0, row_count)
        def _(q):
            wg_send[q] = wg_local[pl.ds(pl.multiple_of(q * chunk, chunk), chunk), :].astype(bf16)

        @pl.loop(1, row_count)
        def _(j):
            w1_copy(j).start()

    for h in range(halves):
        product = dot(pre_grad[...], weight_t[:, h * LANES:(h + 1) * LANES])
        agg_grad[...] = product.astype(bf16)

        def reply(j):
            for c in range(cap):
                chosen = jnp.zeros((B, LANES), f32)
                for b in range(nblk):
                    chosen = jnp.where(is_block(j, c, b), agg_grad[b * B:(b + 1) * B, :].astype(f32), chosen)
                reply_send[h, j, c] = chosen.astype(bf16)

        @pl.loop(1, row_count)
        def _(j):
            reply(j)
            reply_copy(h, j).start()

        reply(0)
        backs[h][pl.ds(pl.multiple_of(r * cap, cap), cap)] = reply_send[h, 0]
        if h == 0:
            wg_first()


    pieces, high, wide = wg_pieces.shape
    scatter = pieces > 1

    def corner(i):
        return corner_of(i, wg_local.shape[1], high, wide)

    def w2_copy(j):
        src = wg_pieces.at[dom_at(j) if scatter else 0]
        return remote(src, wg_dom.at[j], w2_ss.at[j], w2_rs.at[j], (dom_at(j), r))

    def w3_copy(j):
        return remote(wg_mine.at[d], wg_mine.at[d], w3_ss.at[j], w3_rs.at[j], (dom_at(j), r))

    def w4_copy(i, j):
        at = dom_at(-i) if scatter else 0
        return remote(wg_mine.at[at], wg_out.at[r, at], w4_ss.at[i, j], w4_rs.at[i, j], (d, row_at(j)))

    def w4_start(i):
        @pl.loop(1, row_count)
        def _(j):
            w4_copy(i, j).start()

    wg_copy = pltpu.make_async_copy(wg_mine, wg_out.at[r], out_sem.at[1 + halves])

    def wg_second():
        wg_chunk[...] = wg_local[pl.ds(pl.multiple_of(r * chunk, chunk), chunk), :]

        @pl.loop(1, row_count)
        def _(j):
            w1_copy(j).wait_recv()
            wg_chunk[...] += wg_rows[j].astype(f32)

        for i in range(pieces):
            wg_pieces[i] = wg_chunk[corner(i)].astype(bf16)

        @pl.loop(1, dom_count)
        def _(j):
            w2_copy(j).start()

    def g_copy(h, role):
        device = {NEAR: up_dev, FAR: down_dev, MATE: mate_dev, PASSED: mate_dev}[role]
        target = g_recv.at[h] if role == PASSED else grad_out.at[h, role - 1]
        return remote(g_send.at[h, role], target, g_ss.at[h, role], g_rs.at[h, role], device)

    def own_copy(h):
        return pltpu.make_async_copy(g_own.at[h], own_out.at[h], out_sem.at[1 + h])

    for h in range(halves):
        @pl.loop(1, row_count)
        def _(j):
            reply_copy(h, j).wait_recv()

        def source_terms(role, target, extra=None):
            products(tiles_t, backs[h], slot_ref, role)

            @pl.loop(0, nblk)
            def _(b):
                rows = pl.ds(pl.multiple_of(b * B, B), B)
                value = mixed(source_ref, role, b)
                if extra is not None:
                    value = value + extra[rows, :].astype(f32)
                target[rows, :] = value.astype(target.dtype)

        for role in (PASSED, FAR):
            source_terms(role, g_send.at[h, role])
            g_copy(h, role).start()
        g_copy(h, PASSED).wait_recv()
        source_terms(NEAR, g_send.at[h, NEAR], g_recv.at[h])
        g_copy(h, NEAR).start()
        source_terms(MATE, g_send.at[h, MATE])
        g_copy(h, MATE).start()
        source_terms(OWN, g_own.at[h])
        own_copy(h).start()
        if h == 0:
            wg_second()

    if scatter:
        total_own = wg_pieces[d].astype(f32)
        for j in range(1, dom_count):
            w2_copy(j).wait_recv()
            total_own = total_own + wg_dom[j].astype(f32)
        wg_mine[d] = total_own.astype(bf16)

        @pl.loop(1, dom_count)
        def _(j):
            w3_copy(j).start()

        w4_start(0)

        @pl.loop(1, dom_count)
        def _(j):
            w3_copy(j).wait_recv()
            w4_start(j)

        @pl.loop(1, dom_count)
        def _(j):
            w3_copy(j).wait_send()
    else:
        wg_dom[0] = wg_pieces[0]

        @pl.loop(1, dom_count)
        def _(j):
            w2_copy(j).wait_recv()

        wg_mine[0] = lax.fori_loop(
            0, dom_count, lambda i, value: value + wg_dom[dom_at(-i)].astype(f32), jnp.zeros(wg_chunk.shape, f32)
        ).astype(bf16)
        w4_start(0)

    wg_copy.start()

    for h in range(halves):
        for role in (MATE, NEAR, FAR):
            g_copy(h, role).wait_recv()

    @pl.loop(0, dom_count if scatter else 1)
    def _(i):
        @pl.loop(1, row_count)
        def _(j):
            w4_copy(i, j).wait()


    act_copy.wait()
    wg_copy.wait()
    for h in range(halves):
        for role in (NEAR, FAR, MATE, PASSED):
            feat_copy(h, role).wait_send()
            g_copy(h, role).wait_send()
        own_copy(h).wait()

        @pl.loop(1, row_count)
        def _(j):
            part_copy(h, j).wait_send()
            reply_copy(h, j).wait_send()

    @pl.loop(1, row_count)
    def _(j):
        w1_copy(j).wait_send()

    @pl.loop(1, dom_count)
    def _(j):
        w2_copy(j).wait_send()


def corner_of(i, channels, high, wide):
    across = channels // wide
    row, column = i // across * high, i % across * wide
    return slice(row, row + high), slice(column, column + wide)


def hand_over(act, own, grad, wg, to_act, to_grad, to_wg, in_act, in_own, in_grad, in_wg, sums, full, sem, out_sem):
    halves = own.shape[0]
    row_count, pieces, high, wide = wg.shape
    channels = full.shape[0]
    reads = []
    for h in range(halves):
        reads.append(pltpu.make_async_copy(own.at[h], in_own.at[h], sem.at[2 * h]))
        reads.append(pltpu.make_async_copy(grad.at[h], in_grad.at[h], sem.at[2 * h + 1]))
    reads.append(pltpu.make_async_copy(act, in_act, sem.at[2 * halves]))
    reads.append(pltpu.make_async_copy(wg, in_wg, sem.at[2 * halves + 1]))
    for copy in reads:
        copy.start()
    writes = []
    for h in range(halves):
        reads[2 * h].wait()
        reads[2 * h + 1].wait()
        value = in_own[h]
        for i in (2, 0, 1):
            value = value + in_grad[h, i].astype(f32)
        sums[h] = value.astype(bf16)
        writes.append(pltpu.make_async_copy(sums.at[h], to_grad.at[:, pl.ds(h * LANES, LANES)], out_sem.at[h]))
        writes[-1].start()
    reads[-2].wait()
    writes.append(pltpu.make_async_copy(in_act, to_act, out_sem.at[halves]))
    writes[-1].start()
    reads[-1].wait()
    chunk = channels // row_count
    for q in range(row_count):
        for i in range(pieces):
            rows, cols = corner_of(i, channels, high, wide)
            full[q * chunk + rows.start:q * chunk + rows.stop, cols] = in_wg[q, i].astype(f32)
    writes.append(pltpu.make_async_copy(full, to_wg, out_sem.at[halves + 1]))
    writes[-1].start()
    for copy in writes:
        copy.wait()


def per_device(
    features, weight, tile_values, tile_source, tile_slot, slot_block, tile_count, cotangent, *, dom_count, row_count
):
    nodes, channels = features.shape
    nblk = nodes // B
    halves = channels // LANES
    tps = tile_values.shape[2]
    slots = slot_block.shape[1]
    cap = slots // row_count
    chunk = channels // row_count
    scatter = chunk % 16 == 0 and chunk // 16 * halves == dom_count
    pieces, piece = (dom_count, (16, LANES)) if scatter else (1, (chunk, channels))
    smem = pl.BlockSpec(memory_space=pltpu.SMEM)
    anywhere = pl.BlockSpec(memory_space=pl.ANY)
    V = pltpu.VMEM
    dma = pltpu.SemaphoreType.DMA
    scratch = [
        V(tile_values.shape[1:], bf16), V(tile_values.shape[1:], bf16), V(weight.shape, bf16), V(weight.shape[::-1], bf16), V(cotangent.shape, bf16),
        V((tps, B, LANES), f32), V((slots, B, LANES), f32),
        *[V((nblk, B, LANES), bf16) for _ in range(10)],
        V((row_count, cap, 8, LANES), jnp.int32), V((row_count, cap, 8, LANES), jnp.int32),
        V((halves, row_count, cap * B, LANES), bf16), V((halves, row_count, cap * B, LANES), bf16),
        V((halves, nodes, LANES), bf16), V((nodes, channels), f32), V((nodes, channels), bf16), V((nodes, LANES), bf16),
        V((halves, row_count, cap, B, LANES), bf16), V((slots, B, LANES), bf16), V((slots, B, LANES), bf16),
        V((halves, nodes, LANES), f32), V((halves, 5, nodes, LANES), bf16), V((halves, nodes, LANES), bf16),
        V((channels, channels), f32), V((row_count, chunk, channels), bf16), V((row_count, chunk, channels), bf16),
        V((chunk, channels), f32), V((pieces, *piece), bf16), V((dom_count, *piece), bf16), V((pieces, *piece), bf16),
        V((nodes, channels), bf16),
        dma((3 + halves,)), dma((halves, 5)), dma((halves, 5)), dma((row_count,)), dma((row_count,)),
        dma((halves, row_count)), dma((halves, row_count)), dma((halves, row_count)), dma((halves, row_count)),
        dma((halves, 5)), dma((halves, 5)),
        dma((row_count,)), dma((row_count,)), dma((dom_count,)), dma((dom_count,)),
        dma((dom_count,)), dma((dom_count,)), dma((dom_count, row_count)), dma((dom_count, row_count)), dma((2 + halves,)),
    ]
    results = pl.pallas_call(
        functools.partial(kernel, dom_count, row_count),
        out_shape=(
            jax.ShapeDtypeStruct((nodes, channels), bf16),
            jax.ShapeDtypeStruct((halves, nodes, LANES), f32),
            jax.ShapeDtypeStruct((halves, 3, nodes, LANES), bf16),
            jax.ShapeDtypeStruct((row_count, pieces, *piece), bf16),
        ),
        in_specs=[anywhere, anywhere, anywhere, smem, smem, smem, smem, anywhere],
        out_specs=(anywhere,) * 4,
        scratch_shapes=scratch,
        compiler_params=pltpu.CompilerParams(
            collective_id=0, has_side_effects=True, vmem_limit_bytes=56 * 1024 * 1024
        ),
        name="graph_layer",
    )(
        features.reshape(nblk, B, channels), weight, tile_values,
        jnp.swapaxes(tile_source, 1, 2), jnp.swapaxes(tile_slot, 1, 2), slot_block, tile_count, cotangent,
    )
    return pl.pallas_call(
        hand_over,
        out_shape=(
            jax.ShapeDtypeStruct((nodes, channels), bf16),
            jax.ShapeDtypeStruct((nodes, channels), bf16),
            jax.ShapeDtypeStruct((channels, channels), f32),
        ),
        in_specs=[anywhere] * 4,
        out_specs=(anywhere,) * 3,
        scratch_shapes=[
            *[V(x.shape, x.dtype) for x in results],
            V((halves, nodes, LANES), bf16), V((channels, channels), f32), dma((2 * halves + 2,)), dma((halves + 2,)),
        ],
        compiler_params=pltpu.CompilerParams(vmem_limit_bytes=60 * 1024 * 1024),
        name="hand_over",
    )(*results)


def solution(mesh):
    both = P(("dom", "rows"))
    return jax.shard_map(
        functools.partial(per_device, dom_count=mesh.shape["dom"], row_count=mesh.shape["rows"]),
        mesh=mesh,
        in_specs=(both, P(), both, both, both, both, both, both),
        out_specs=(both, both, P()),
        check_vma=False,
    )
```
